512 devices in a mesh: blk: 64 (over z_hi, y, core), group: 8 (over z_lo, x).
Axes of the slice: x: 4, y: 8, z: 8 (z_hi: 4, z_lo: 2; z = z_hi * 2 + z_lo), core: 2. Of those that a mesh axis runs over, the one named last changes fastest.
Arguments:
- image_rows: bfloat16 [65536, 768], P(('blk', 'group')), may hold values from -0.59765625 to 0.59765625
- text_rows: bfloat16 [65536, 768], P(('blk', 'group')), may hold values from -0.59765625 to 0.59765625
- log_norm: float32 [65536], P(('blk', 'group'))
- row_grad: float32 [65536], P(('blk', 'group')), may hold values from 0.25 to 2
- pos_index: int32 [65536], P(('blk', 'group')), may hold values from 0 to 1023
- logit_scale: float32 [], replicated, may hold values from 10 to 16
Outputs:
- image_grad: bfloat16 [65536, 768], P(('blk', 'group'))
- text_grad: bfloat16 [65536, 768], P(('blk', 'group'))
The draws below stay inside these ranges and needn't reach their ends.
Inputs may be any that keep to these rules, and one draw needn't show every extreme that they name: `pos_index`: the positive text lies in the image row's own block.
All inputs are finite; a program needn't handle non-finite values.
Results may differ from the reference program's by a relative error of at most 0.015.
Values may be sent and summed in bfloat16 or wider, within the bound.
A program may use at most 64 MiB of HBM per device.

```python
import jax
import jax.numpy as jnp
from jax import lax

D = 768
ROWS = 128
WINDOW = 4
BLOCK = 1024
TOTAL = 65536
N_BLK = 64
N_GROUP = 8


def draw_log_norm(key, part):
    key = jax.random.fold_in(key, 7)
    spread = jax.random.uniform(key, (TOTAL,), jnp.float32, -1.0, 1.0)
    return jnp.log(1.0 * WINDOW * BLOCK) + 0.5 * (13.0 * 0.0064) ** 2 * D + spread


def place_ends(values, stream_key, least, top_value):
    longest = values.shape.index(max(values.shape))
    spots = []
    for shift in (0, 1):
        where = [jax.random.randint(jax.random.fold_in(stream_key, axis), (), 0, length) for axis, length in enumerate(values.shape)]
        where[longest] = (where[longest] + shift) % values.shape[longest]
        spots.append(tuple(where))
    return values.at[spots[0]].set(least).at[spots[1]].set(top_value)


def block_scale(rng, dims, split, least, largest):
    factor_of = 1.0
    for dim, parts in split:
        steps = jax.random.uniform(jax.random.fold_in(jax.random.fold_in(rng, 6), dim), (parts,), jnp.float32, least / len(split), largest / len(split))
        factor_of = factor_of * jnp.repeat(jnp.exp(steps), dims[dim] // parts).reshape((-1,) + (1,) * (len(dims) - 1 - dim))
    return factor_of


def noise(stream_key, dims, scale, most, pieces=(), kind=jnp.bfloat16):
    values = scale * jax.random.normal(stream_key, dims, jnp.float32)
    if pieces:
        values = values * block_scale(stream_key, dims, pieces, -0.22, 0.18)
    return jnp.clip(values, -most, most).astype(kind)


def setup_inputs(seed: int = 0) -> dict:
    keys = jax.random.split(jax.random.key(seed), 7)
    return {
        "image_rows": noise(keys[0], (TOTAL, D), 0.08, 0.59765625, ((0, 512),)),
        "text_rows": noise(keys[1], (TOTAL, D), 0.08, 0.59765625, ((0, 512),)),
        "log_norm": draw_log_norm(jax.random.fold_in(keys[6], 71), 0),
        "row_grad": jnp.clip(0.25 + 1.75 * jax.random.uniform(keys[3], (TOTAL,), jnp.float32) ** block_scale(keys[3], (TOTAL,), ((0, 512),), -0.2, 0.2), 0.25, 2.0),
        "pos_index": place_ends(jax.random.randint(keys[4], (TOTAL,), 0, BLOCK), jax.random.fold_in(keys[4], 1), 0, BLOCK - 1).astype(jnp.int32),
        "logit_scale": jnp.clip(jax.random.uniform(keys[5], (), jnp.float32, 10.0, 16.0), 10.0, 16.0),
    }


def weigh_rows(image_part, text_part, log_part, grad_part, pos_part, logit_scale, with_pos):
    scores = jnp.einsum("grd,jd->grj", image_part.astype(jnp.float32), text_part.astype(jnp.float32))
    row_prob = jnp.exp(logit_scale * scores - log_part[..., None])
    if with_pos:
        column = jnp.arange(text_part.shape[0], dtype=jnp.int32)
        row_prob = row_prob - (column == pos_part[..., None]).astype(jnp.float32)
    return (row_prob * (logit_scale * grad_part)[..., None]).astype(jnp.bfloat16)


def reference(image_rows, text_rows, log_norm, row_grad, pos_index, logit_scale):
    images_split = image_rows.reshape(N_BLK, N_GROUP, ROWS, D)
    texts_split = text_rows.reshape(N_BLK, BLOCK, D)
    logs_split = log_norm.reshape(N_BLK, N_GROUP, ROWS)
    grads_split = row_grad.reshape(N_BLK, N_GROUP, ROWS)
    pos_split = pos_index.reshape(N_BLK, N_GROUP, ROWS)

    def image_side(block):
        total = jnp.zeros((N_GROUP, ROWS, D), jnp.float32)
        for offset in range(WINDOW):
            source = (block - offset) % N_BLK
            text_part = texts_split[source]
            weight = weigh_rows(images_split[block], text_part, logs_split[block], grads_split[block], pos_split[block], logit_scale, offset == 0)
            total = total + jnp.einsum("grj,jd->grd", weight.astype(jnp.float32), text_part.astype(jnp.float32))
        return total.astype(jnp.bfloat16)

    def text_side(block):
        partial_value = jnp.zeros((N_GROUP, BLOCK, D), jnp.bfloat16)
        for offset in range(WINDOW):
            source = (block + offset) % N_BLK
            weight = weigh_rows(images_split[source], texts_split[block], logs_split[source], grads_split[source], pos_split[source], logit_scale, offset == 0)
            term = jnp.einsum("grj,grd->gjd", weight.astype(jnp.float32), images_split[source].astype(jnp.float32))
            if offset == 0:
                partial_value = term.astype(jnp.bfloat16)
            else:
                partial_value = (partial_value.astype(jnp.float32) + term).astype(jnp.bfloat16)
        return jnp.sum(partial_value.astype(jnp.float32), axis=0).astype(jnp.bfloat16)

    blocks = jnp.arange(N_BLK, dtype=jnp.int32)
    image_grad = lax.map(image_side, blocks).reshape(TOTAL, D)
    text_grad = lax.map(text_side, blocks).reshape(TOTAL, D)
    return (image_grad, text_grad)
```

```python
import functools

import jax
import jax.numpy as jnp
from jax import lax
from jax.experimental import pallas as pl
from jax.experimental.pallas import tpu as pltpu
from jax.sharding import PartitionSpec as P

MESH = pl.DeviceIdType.MESH
WINDOW = 4
F32 = jnp.float32
BF16 = jnp.bfloat16

(T_NEXT, T_FAR, T_SIDE, T_CORE, T_CORE_SIDE, T_PASS, T_PASS_SIDE, T_HOP, T_HOP_FAR) = range(9)
IMG = 9
PRM = 12
(G_CORE, G_CORE_OWN, G_SIDE_OWN, G_SIDE_BACK, G_SIDE_FAR, G_BACK, G_FAR) = range(15, 22)
IGR = 22
N_COPIES = 25


def kernel(n_blk, scale_ref, image_ref, text_ref, log_ref, grad_ref, pos_ref, image_out, text_out,
           img, prm, tx, rowv, posv, w, tg, ig, core_out, core_in, side_out, side_in, far_out, far_in,
           img_out, img_in, load_sem, send_sem, recv_sem):
    rows = image_ref.shape[0]
    blk, grp = lax.axis_index("blk"), lax.axis_index("group")
    c = blk % 2
    pair = blk // 2
    n_pair = n_blk // 2
    z, x = grp // 4, grp % 4
    x_a = x + 1 - 2 * (x % 2)
    x_b = 3 - x

    def at_pair(step, core):
        return ((pair + step + n_pair) % n_pair) * 2 + core

    core_dev = (pair * 2 + 1 - c, grp)
    side_dev = (blk, z * 4 + x_b)
    img_devs = ((blk, z * 4 + x_a), (blk, (1 - z) * 4 + x), (blk, (1 - z) * 4 + x_a))
    next_dev = (at_pair(1, c), grp)
    back_dev = (at_pair(-1, c), grp)
    far_dev = (at_pair(4 * c - 2, 1 - c), grp)

    own, side = pl.ds(0, rows), pl.ds(rows, rows)

    def copy(index, src, dst, device):
        return pltpu.make_async_remote_copy(
            src_ref=src, dst_ref=dst, send_sem=send_sem.at[index], recv_sem=recv_sem.at[index],
            device_id=device, device_id_type=MESH,
        )

    loads = [
        pltpu.make_async_copy(text_ref, tx.at[0, own], load_sem.at[0]),
        pltpu.make_async_copy(image_ref, img.at[own], load_sem.at[1]),
        pltpu.make_async_copy(log_ref, rowv.at[0], load_sem.at[2]),
        pltpu.make_async_copy(grad_ref, rowv.at[1], load_sem.at[3]),
        pltpu.make_async_copy(pos_ref, posv, load_sem.at[4]),
    ]
    for load in loads:
        load.start()

    barrier = pltpu.get_barrier_semaphore()
    partners = (core_dev, side_dev, *img_devs, next_dev, back_dev, far_dev)
    for device in partners:
        pl.semaphore_signal(barrier, inc=1, device_id=device, device_id_type=MESH)
    for load in loads:
        load.wait()
    prm[0:1, 0:rows] = rowv[0]
    prm[1:2, 0:rows] = rowv[1]
    prm[2:3, 0:rows] = posv[...].astype(F32)
    prm[3:8, 0:rows] = jnp.zeros((5, rows), F32)
    pl.semaphore_wait(barrier, len(partners))

    scale = scale_ref[0, 0]
    base_own = (grp * rows).astype(F32)
    base_side = ((z * 4 + x_b) * rows).astype(F32)

    t_next = copy(T_NEXT, tx.at[0, own], tx.at[2, own], next_dev)
    t_far = copy(T_FAR, tx.at[0, own], tx.at[3, own], far_dev)
    t_side = copy(T_SIDE, tx.at[0, own], tx.at[0, side], side_dev)
    t_core = copy(T_CORE, tx.at[0, own], tx.at[1, own], core_dev)
    t_core_side = copy(T_CORE_SIDE, tx.at[0, side], tx.at[1, side], core_dev)
    pass_slot = 3 - 2 * c
    get_slot = 1 + 2 * c
    t_pass = copy(T_PASS, tx.at[2, own], tx.at[pass_slot, own], core_dev)
    t_pass_side = copy(T_PASS_SIDE, tx.at[2, side], tx.at[pass_slot, side], core_dev)
    t_hop = copy(T_HOP, tx.at[2, own], tx.at[2, side], side_dev)
    t_hop_far = copy(T_HOP_FAR, tx.at[3, own], tx.at[3, side], side_dev)
    images = [copy(IMG + i, img.at[own], img.at[pl.ds((i + 1) * rows, rows)], img_devs[i]) for i in range(3)]
    params = [copy(PRM + i, prm.at[:, own], prm.at[:, pl.ds((i + 1) * rows, rows)], img_devs[i]) for i in range(3)]
    g_core = copy(G_CORE, core_out.at[0], core_in.at[0], core_dev)
    g_core_own = copy(G_CORE_OWN, core_out.at[1], core_in.at[1], core_dev)
    g_side_own = copy(G_SIDE_OWN, side_out.at[0], side_in.at[0], side_dev)
    g_side_back = copy(G_SIDE_BACK, side_out.at[1], side_in.at[1], side_dev)
    g_side_far = copy(G_SIDE_FAR, side_out.at[2], side_in.at[2], side_dev)
    g_back = copy(G_BACK, far_out.at[0], far_in.at[0], back_dev)
    g_far = copy(G_FAR, far_out.at[1], far_in.at[1], far_dev)
    image_back = [copy(IGR + i, img_out.at[i], img_in.at[i], img_devs[i]) for i in range(3)]

    t_next.start()
    pl.when(c == 1)(t_far.start)
    t_side.start()
    pl.when(c == 0)(t_core.start)
    for i in (2, 0, 1):
        images[i].start()
        params[i].start()

    t_side.wait_recv()
    pl.when(c == 0)(t_core_side.start)
    t_next.wait_recv()
    t_hop.start()
    t_pass.start()

    @pl.when(c == 0)
    def _():
        t_far.wait_recv()
        t_hop_far.start()

    for i in range(3):
        params[i].wait_recv()
        images[i].wait_recv()

    def step_body(s, _):
        later = 1 + s % 3
        k = c * s + (1 - c) * ((s + 2) // 3) * later

        @pl.when((s == 1) & (c == 0))
        def _():
            t_hop.wait_recv()
            t_pass_side.start()

        @pl.when((s == 2) & (c == 0))
        def _():
            t_hop_far.wait_recv()

        @pl.when((s == 1) & (c == 1))
        def _():
            t_core.wait_recv()
            t_core_side.wait_recv()

        @pl.when((s == 2) & (c == 1))
        def _():
            t_hop.wait_recv()
            t_pass_side.start()

        @pl.when(s == 3)
        def _():
            t_pass.wait_recv()
            t_pass_side.wait_recv()

        text = tx[k]
        scores = lax.dot_general(text, img[...], (((1,), (1,)), ((), ())), preferred_element_type=F32)
        prob = jnp.exp(scale * scores - prm[0:1, :])
        row = lax.broadcasted_iota(jnp.int32, scores.shape, 0)
        place = jnp.where(row < rows, row.astype(F32) + base_own, (row - rows).astype(F32) + base_side)
        place = place + (k * 65536).astype(F32)
        prob = prob - jnp.where(place == prm[2:3, :], 1.0, 0.0)
        w[...] = (prob * (scale * prm[1:2, :])).astype(BF16)
        tg[k] = jnp.dot(w[...], img[...], preferred_element_type=F32)

        @pl.when((s == 0) & (c == 1))
        def _():
            side_out[0] = tg[0, side].astype(BF16)
            g_side_own.start()

        @pl.when((s == 1) & (c == 1))
        def _():
            core_out[1] = tg[1].astype(BF16)
            g_core_own.start()

        @pl.when((s == 2) & (c == 0))
        def _():
            side_out[2] = tg[3, side].astype(BF16)
            g_side_far.start()

        @pl.when(s == 3)
        def _():
            core_out[0] = tg[k].astype(BF16)
            g_core.start()

        term = lax.dot_general(w[...], tx[k], (((0,), (0,)), ((), ())), preferred_element_type=F32)

        @pl.when(s == 0)
        def _():
            ig[...] = term

        @pl.when(s > 0)
        def _():
            ig[...] += term

        return 0

    lax.fori_loop(0, WINDOW, step_body, 0)

    for i in (2, 0, 1):
        img_out[i] = ig[(i + 1) * rows:(i + 2) * rows].astype(BF16)
        image_back[i].start()

    g_core.wait_recv()
    side_out[1] = (tg[2, side] + core_in[0, side].astype(F32)).astype(BF16)
    g_side_back.start()

    @pl.when(c == 0)
    def _():
        g_core_own.wait_recv()
        side_out[0] = (tg[0, side] + core_in[1, side].astype(F32)).astype(BF16)
        g_side_own.start()
        tg[0, own] += core_in[1, own].astype(F32)
        g_side_far.wait_recv()
        far_out[1] = (tg[3, own] + side_in[2].astype(F32)).astype(BF16)
        g_far.start()

    tg[2, own] += core_in[0, own].astype(F32)
    g_side_back.wait_recv()
    far_out[0] = (tg[2, own] + side_in[1].astype(F32)).astype(BF16)
    g_back.start()
    g_side_own.wait_recv()
    tg[0, own] += side_in[0].astype(F32)

    for i in range(3):
        image_back[i].wait_recv()
    image_out[...] = (
        (ig[own] + img_in[0].astype(F32)) + (img_in[1].astype(F32) + img_in[2].astype(F32))
    ).astype(BF16)

    g_back.wait_recv()

    @pl.when(c == 1)
    def _():
        g_far.wait_recv()
        tg[0, own] += far_in[1].astype(F32)

    text_out[...] = (tg[0, own] + far_in[0].astype(F32)).astype(BF16)

    for sent in (t_next, t_side, t_pass, t_pass_side, t_hop, *images, *params, g_core, g_side_own,
                 g_side_back, g_back, *image_back):
        sent.wait_send()

    @pl.when(c == 0)
    def _():
        for sent in (t_core, t_core_side, t_hop_far, g_side_far, g_far):
            sent.wait_send()

    @pl.when(c == 1)
    def _():
        for sent in (t_far, g_core_own):
            sent.wait_send()


def solution(mesh):
    n_blk = mesh.shape["blk"]

    def per_device(image_rows, text_rows, log_norm, row_grad, pos_index, logit_scale):
        rows, width = image_rows.shape
        block = pltpu.VMEM((rows, width), BF16)
        anywhere = pl.BlockSpec(memory_space=pl.ANY)
        return pl.pallas_call(
            functools.partial(kernel, n_blk),
            out_shape=(jax.ShapeDtypeStruct((rows, width), BF16),) * 2,
            in_specs=[pl.BlockSpec(memory_space=pltpu.SMEM)] + [anywhere] * 5,
            out_specs=(pl.BlockSpec(memory_space=pltpu.VMEM),) * 2,
            scratch_shapes=[
                pltpu.VMEM((4 * rows, width), BF16),
                pltpu.VMEM((8, 4 * rows), F32),
                pltpu.VMEM((WINDOW, 2 * rows, width), BF16),
                pltpu.VMEM((2, 1, rows), F32),
                pltpu.VMEM((1, rows), jnp.int32),
                pltpu.VMEM((2 * rows, 4 * rows), BF16),
                pltpu.VMEM((WINDOW, 2 * rows, width), F32),
                pltpu.VMEM((4 * rows, width), F32),
                pltpu.VMEM((2, 2 * rows, width), BF16),
                pltpu.VMEM((2, 2 * rows, width), BF16),
                pltpu.VMEM((3, rows, width), BF16),
                pltpu.VMEM((3, rows, width), BF16),
                pltpu.VMEM((2, rows, width), BF16),
                pltpu.VMEM((2, rows, width), BF16),
                pltpu.VMEM((3, rows, width), BF16),
                pltpu.VMEM((3, rows, width), BF16),
                pltpu.SemaphoreType.DMA((5,)),
                pltpu.SemaphoreType.DMA((N_COPIES,)),
                pltpu.SemaphoreType.DMA((N_COPIES,)),
            ],
            compiler_params=pltpu.CompilerParams(
                collective_id=0, has_side_effects=True, vmem_limit_bytes=40 * 2**20
            ),
            name="window_loss_grad",
        )(
            logit_scale.reshape(1, 1), image_rows, text_rows, log_norm.reshape(1, rows),
            row_grad.reshape(1, rows), pos_index.reshape(1, rows),
        )

    return jax.shard_map(
        per_device,
        mesh=mesh,
        in_specs=(
            P(("blk", "group"), None),
            P(("blk", "group"), None),
            P(("blk", "group")),
            P(("blk", "group")),
            P(("blk", "group")),
            P(),
        ),
        out_specs=(P(("blk", "group"), None), P(("blk", "group"), None)),
        check_vma=False,
    )
```

```python
import functools

import jax
import jax.numpy as jnp
from jax import lax
from jax.experimental import pallas as pl
from jax.experimental.pallas import tpu as pltpu
from jax.sharding import PartitionSpec as P

MESH = pl.DeviceIdType.MESH
F32 = jnp.float32
BF16 = jnp.bfloat16
PIECES = 2

T_SIDE = 0
T_NEXT = 1
T_HOP = T_NEXT + PIECES
T_FAR = T_HOP + PIECES
T_FAR_HOP = T_FAR + PIECES
IMG = T_FAR_HOP + PIECES
PRM = IMG + 3
IMG_CORE = PRM + 3
PRM_CORE = IMG_CORE + 4
G_SIDE = PRM_CORE + 1
G_HOP = G_SIDE + 1
G_BACK = G_HOP + PIECES
G_FAR_HOP = G_BACK + PIECES
G_FAR = G_FAR_HOP + PIECES
IG_CORE = G_FAR + PIECES
IG = IG_CORE + 4
N_COPIES = IG + 3


def kernel(n_blk, scale_ref, image_ref, text_ref, log_ref, grad_ref, pos_ref, image_out, text_out,
           img, prm, tx, rowv, posv, w, tg, ig, core_out, core_in, side_out, side_in, hop_out, hop_in,
           back_out, back_in, img_out, img_in, load_sem, send_sem, recv_sem):
    rows = image_ref.shape[0]
    piece = rows // PIECES
    blk, grp = lax.axis_index("blk"), lax.axis_index("group")
    c = blk % 2
    pair = blk // 2
    n_pair = n_blk // 2
    z, x = grp // 4, grp % 4
    x_a = x + 1 - 2 * (x % 2)
    x_b = 3 - x

    def at_pair(step):
        return (((pair + step + n_pair) % n_pair) * 2 + c, grp)

    core_dev = (pair * 2 + 1 - c, grp)
    side_dev = (blk, z * 4 + x_b)
    img_devs = ((blk, z * 4 + x_a), (blk, (1 - z) * 4 + x), (blk, (1 - z) * 4 + x_a))
    next_dev, back_dev = at_pair(1), at_pair(-1)
    next2_dev, back2_dev = at_pair(2), at_pair(-2)

    own, side = pl.ds(0, rows), pl.ds(rows, rows)

    def slot(i):
        return pl.ds(i * rows, rows)

    def part(i):
        return pl.ds(i * piece, piece)

    def side_part(i):
        return pl.ds(rows + i * piece, piece)

    def copy(index, src, dst, device):
        return pltpu.make_async_remote_copy(
            src_ref=src, dst_ref=dst, send_sem=send_sem.at[index], recv_sem=recv_sem.at[index],
            device_id=device, device_id_type=MESH,
        )

    loads = [
        pltpu.make_async_copy(text_ref, tx.at[0, own], load_sem.at[0]),
        pltpu.make_async_copy(image_ref, img.at[c, own], load_sem.at[1]),
        pltpu.make_async_copy(log_ref, rowv.at[0], load_sem.at[2]),
        pltpu.make_async_copy(grad_ref, rowv.at[1], load_sem.at[3]),
        pltpu.make_async_copy(pos_ref, posv, load_sem.at[4]),
    ]
    for load in loads:
        load.start()

    barrier = pltpu.get_barrier_semaphore()
    partners = (core_dev, side_dev, *img_devs, next_dev, back_dev, next2_dev, back2_dev)
    for device in partners:
        pl.semaphore_signal(barrier, inc=1, device_id=device, device_id_type=MESH)
    for load in loads:
        load.wait()
    prm[c, 0:1, 0:rows] = rowv[0]
    prm[c, 1:2, 0:rows] = rowv[1]
    prm[c, 2:3, 0:rows] = posv[...].astype(F32)
    prm[c, 3:8, 0:rows] = jnp.zeros((5, rows), F32)
    pl.semaphore_wait(barrier, len(partners))

    scale = scale_ref[0, 0]
    base_own = (grp * rows).astype(F32)
    base_side = ((z * 4 + x_b) * rows).astype(F32)
    two = range(PIECES)

    t_side = copy(T_SIDE, tx.at[0, own], tx.at[0, side], side_dev)
    t_next = [copy(T_NEXT + i, tx.at[0, part(i)], tx.at[1, part(i)], next_dev) for i in two]
    t_hop = [copy(T_HOP + i, tx.at[1, part(i)], tx.at[1, side_part(i)], side_dev) for i in two]
    t_far = [copy(T_FAR + i, tx.at[1, part(i)], tx.at[2, part(i)], next_dev) for i in two]
    t_far_hop = [copy(T_FAR_HOP + i, tx.at[2, part(i)], tx.at[2, side_part(i)], side_dev) for i in two]
    images = [copy(IMG + i, img.at[c, own], img.at[c, slot(i + 1)], img_devs[i]) for i in range(3)]
    params = [copy(PRM + i, prm.at[c, :, own], prm.at[c, :, slot(i + 1)], img_devs[i]) for i in range(3)]
    img_core = [copy(IMG_CORE + i, img.at[c, slot(i)], img.at[c, slot(i)], core_dev) for i in range(4)]
    prm_core = copy(PRM_CORE, prm.at[c], prm.at[c], core_dev)
    img_got = [copy(IMG_CORE + i, img.at[1 - c, slot(i)], img.at[1 - c, slot(i)], core_dev) for i in range(4)]
    prm_got = copy(PRM_CORE, prm.at[1 - c], prm.at[1 - c], core_dev)

    g_side = copy(G_SIDE, side_out, side_in, side_dev)
    g_hop = [copy(G_HOP + i, hop_out.at[0, part(i)], hop_in.at[0, part(i)], side_dev) for i in two]
    g_far_hop = [copy(G_FAR_HOP + i, hop_out.at[1, part(i)], hop_in.at[1, part(i)], side_dev) for i in two]
    g_back = [copy(G_BACK + i, back_out.at[0, part(i)], back_in.at[0, part(i)], back_dev) for i in two]
    g_far = [copy(G_FAR + i, back_out.at[1, part(i)], back_in.at[1, part(i)], back2_dev) for i in two]
    ig_core = [copy(IG_CORE + i, core_out.at[slot(i)], core_in.at[slot(i)], core_dev) for i in range(4)]
    ig_back = [copy(IG + i, img_out.at[i], img_in.at[i], img_devs[i]) for i in range(3)]

    for i in two:
        t_next[i].start()
    for i in (2, 0, 1):
        images[i].start()
        params[i].start()
    t_side.start()
    img_core[0].start()

    for i in two:
        t_next[i].wait_recv()
        pl.when(c == 1)(t_far[i].start)
        t_hop[i].start()
    for i in (0, 1, 2):
        images[i].wait_recv()
        img_core[i + 1].start()
        params[i].wait_recv()
    prm_core.start()

    @pl.when(c == 1)
    def _():
        for i in two:
            t_far[i].wait_recv()
            t_far_hop[i].start()

    t_side.wait_recv()

    def tile(s, _):
        j = (s + 1) // 2 - (s // 3) * (2 - 2 * c)
        i = c + (s // 2) * (1 - 2 * c)

        @pl.when(s == 1)
        def _():
            for q in two:
                t_hop[q].wait_recv()

        @pl.when(s == 2)
        def _():
            for q in range(4):
                img_got[q].wait_recv()
            prm_got.wait_recv()

        @pl.when((s == 3) & (c == 1))
        def _():
            for q in two:
                t_far_hop[q].wait_recv()

        scores = lax.dot_general(tx[j], img[i], (((1,), (1,)), ((), ())), preferred_element_type=F32)
        prob = jnp.exp(scale * scores - prm[i, 0:1, :])
        row = lax.broadcasted_iota(jnp.int32, scores.shape, 0)
        place = jnp.where(row < rows, row.astype(F32) + base_own, (row - rows).astype(F32) + base_side)
        place = place + (s * 65536).astype(F32)
        prob = prob - jnp.where(place == prm[i, 2:3, :], 1.0, 0.0)
        w[...] = (prob * (scale * prm[i, 1:2, :])).astype(BF16)
        term = jnp.dot(w[...], img[i], preferred_element_type=F32)
        fresh = (s < 2) | ((s == 3) & (c == 1))

        @pl.when(fresh)
        def _():
            tg[j] = term

        @pl.when(jnp.logical_not(fresh))
        def _():
            tg[j] += term

        @pl.when(((s == 0) & (c == 1)) | ((s == 3) & (c == 0)))
        def _():
            side_out[...] = tg[0, side].astype(BF16)
            g_side.start()

        @pl.when(s == 2)
        def _():
            for q in two:
                hop_out[0, part(q)] = tg[1, side_part(q)].astype(BF16)
                g_hop[q].start()

        @pl.when((s == 3) & (c == 1))
        def _():
            for q in two:
                hop_out[1, part(q)] = tg[2, side_part(q)].astype(BF16)
                g_far_hop[q].start()

        back = lax.dot_general(w[...], tx[j], (((0,), (0,)), ((), ())), preferred_element_type=F32)

        @pl.when(s % 2 == 0)
        def _():
            ig[i] = back

        @pl.when(s % 2 == 1)
        def _():
            ig[i] += back

        return 0

    lax.fori_loop(0, 4, tile, 0)

    for i in (3, 1, 2, 0):
        core_out[slot(i)] = ig[1 - c, slot(i)].astype(BF16)
        ig_core[i].start()

    for i in (3, 1, 2):
        ig_core[i].wait_recv()
        img_out[i - 1] = (ig[c, slot(i)] + core_in[slot(i)].astype(F32)).astype(BF16)
        ig_back[i - 1].start()

    for i in two:
        g_hop[i].wait_recv()
        back_out[0, part(i)] = (tg[1, part(i)] + hop_in[0, part(i)].astype(F32)).astype(BF16)
        g_back[i].start()

    @pl.when(c == 1)
    def _():
        for i in two:
            g_far_hop[i].wait_recv()
            back_out[1, part(i)] = (tg[2, part(i)] + hop_in[1, part(i)].astype(F32)).astype(BF16)
            g_far[i].start()

    ig_core[0].wait_recv()
    ig[c, own] += core_in[own].astype(F32)
    g_side.wait_recv()
    tg[0, own] += side_in[...].astype(F32)

    for i in range(3):
        ig_back[i].wait_recv()
    image_out[...] = (
        (ig[c, own] + img_in[0].astype(F32)) + (img_in[1].astype(F32) + img_in[2].astype(F32))
    ).astype(BF16)

    for i in two:
        g_back[i].wait_recv()

    @pl.when(c == 0)
    def _():
        text_out[...] = (tg[0, own] + back_in[0].astype(F32)).astype(BF16)

    @pl.when(c == 1)
    def _():
        for i in two:
            g_far[i].wait_recv()
        text_out[...] = ((tg[0, own] + back_in[0].astype(F32)) + back_in[1].astype(F32)).astype(BF16)

    for sent in (t_side, *t_next, *t_hop, *images, *params, *img_core, prm_core, g_side, *g_hop, *g_back,
                 *ig_core, *ig_back):
        sent.wait_send()

    @pl.when(c == 1)
    def _():
        for sent in (*t_far, *t_far_hop, *g_far_hop, *g_far):
            sent.wait_send()


def solution(mesh):
    n_blk = mesh.shape["blk"]

    def per_device(image_rows, text_rows, log_norm, row_grad, pos_index, logit_scale):
        rows, width = image_rows.shape
        anywhere = pl.BlockSpec(memory_space=pltpu.HBM)
        return pl.pallas_call(
            functools.partial(kernel, n_blk),
            out_shape=(jax.ShapeDtypeStruct((rows, width), BF16),) * 2,
            in_specs=[pl.BlockSpec(memory_space=pltpu.SMEM)] + [anywhere] * 5,
            out_specs=(pl.BlockSpec(memory_space=pltpu.VMEM),) * 2,
            scratch_shapes=[
                pltpu.VMEM((2, 4 * rows, width), BF16),
                pltpu.VMEM((2, 8, 4 * rows), F32),
                pltpu.VMEM((3, 2 * rows, width), BF16),
                pltpu.VMEM((2, 1, rows), F32),
                pltpu.VMEM((1, rows), jnp.int32),
                pltpu.VMEM((2 * rows, 4 * rows), BF16),
                pltpu.VMEM((3, 2 * rows, width), F32),
                pltpu.VMEM((2, 4 * rows, width), F32),
                pltpu.VMEM((4 * rows, width), BF16),
                pltpu.VMEM((4 * rows, width), BF16),
                pltpu.VMEM((rows, width), BF16),
                pltpu.VMEM((rows, width), BF16),
                pltpu.VMEM((2, rows, width), BF16),
                pltpu.VMEM((2, rows, width), BF16),
                pltpu.VMEM((2, rows, width), BF16),
                pltpu.VMEM((2, rows, width), BF16),
                pltpu.VMEM((3, rows, width), BF16),
                pltpu.VMEM((3, rows, width), BF16),
                pltpu.SemaphoreType.DMA((5,)),
                pltpu.SemaphoreType.DMA((N_COPIES,)),
                pltpu.SemaphoreType.DMA((N_COPIES,)),
            ],
            compiler_params=pltpu.CompilerParams(
                collective_id=0, has_side_effects=True, vmem_limit_bytes=40 * 2**20
            ),
            name="window_loss_grad",
        )(
            logit_scale.reshape(1, 1), image_rows, text_rows, log_norm.reshape(1, rows),
            row_grad.reshape(1, rows), pos_index.reshape(1, rows),
        )

    return jax.shard_map(
        per_device,
        mesh=mesh,
        in_specs=(
            P(("blk", "group"), None),
            P(("blk", "group"), None),
            P(("blk", "group")),
            P(("blk", "group")),
            P(("blk", "group")),
            P(),
        ),
        out_specs=(P(("blk", "group"), None), P(("blk", "group"), None)),
        check_vma=False,
    )
```

```python
import functools

import jax
import jax.numpy as jnp
from jax import lax
from jax.experimental import pallas as pl
from jax.experimental.pallas import tpu as pltpu
from jax.sharding import PartitionSpec as P

MESH = pl.DeviceIdType.MESH
F32 = jnp.float32
BF16 = jnp.bfloat16
PIECES = 2
Y = 8

T_SIDE = 0
T_NEXT = 1
T_HOP = T_NEXT + PIECES
T_FAR = T_HOP + PIECES
T_FAR_HOP = T_FAR + PIECES
IMG = T_FAR_HOP + PIECES
IMG_Z = IMG + 1
IMG_AZ = IMG_Z + PIECES
PRM = IMG_AZ + PIECES
IMG_CORE = PRM + 3
PRM_CORE = IMG_CORE + 4
G_SIDE = PRM_CORE + 1
G_HOP = G_SIDE + 1
G_BACK = G_HOP + PIECES
G_FAR_HOP = G_BACK + PIECES
G_FAR = G_FAR_HOP + PIECES
IG_CORE = G_FAR + PIECES
IG = IG_CORE + 4
T_RELAY = IG + 3
G_RELAY = T_RELAY + 1
N_COPIES = G_RELAY + 1


def kernel(n_blk, scale_ref, image_ref, text_ref, log_ref, grad_ref, pos_ref, image_out, text_out,
           img, prm, tx, rowv, posv, w, tg, ig, core_out, core_in, side_out, side_in, hop_out, hop_in,
           back_out, back_in, img_out, img_in, relay, load_sem, send_sem, recv_sem, ready):
    rows = image_ref.shape[0]
    piece = rows // PIECES
    blk, grp = lax.axis_index("blk"), lax.axis_index("group")
    c = blk % 2
    pair = blk // 2
    n_pair = n_blk // 2
    z, x = grp // 4, grp % 4
    x_a = x + 1 - 2 * (x % 2)
    x_b = 3 - x

    def at_pair(step):
        return (((pair + step + n_pair) % n_pair) * 2 + c, grp)

    core_dev = (pair * 2 + 1 - c, grp)
    side_dev = (blk, z * 4 + x_b)
    a_dev, z_dev = (blk, z * 4 + x_a), (blk, (1 - z) * 4 + x)
    img_devs = (a_dev, z_dev, (blk, (1 - z) * 4 + x_a))
    next_dev, back_dev = at_pair(1), at_pair(-1)
    back2_dev = at_pair(-2)
    y = pair % Y
    last, first = y == Y - 1, y == 0
    z_next, z_back = at_pair(Y), at_pair(-Y)
    y_next, y_back = at_pair((y + 1) % Y - y), at_pair((y + Y - 1) % Y - y)

    own, side = pl.ds(0, rows), pl.ds(rows, rows)

    def slot(i):
        return pl.ds(i * rows, rows)

    def part(i):
        return pl.ds(i * piece, piece)

    def slot_part(s, i):
        return pl.ds(s * rows + i * piece, piece)

    def side_part(i):
        return slot_part(1, i)

    def copy(index, src, dst, device):
        return pltpu.make_async_remote_copy(
            src_ref=src, dst_ref=dst, send_sem=send_sem.at[index], recv_sem=recv_sem.at[index],
            device_id=device, device_id_type=MESH,
        )

    loads = [
        pltpu.make_async_copy(text_ref, tx.at[0, own], load_sem.at[0]),
        pltpu.make_async_copy(image_ref, img.at[c, own], load_sem.at[1]),
        pltpu.make_async_copy(log_ref, rowv.at[0], load_sem.at[2]),
        pltpu.make_async_copy(grad_ref, rowv.at[1], load_sem.at[3]),
        pltpu.make_async_copy(pos_ref, posv, load_sem.at[4]),
    ]
    for load in loads:
        load.start()

    barrier = pltpu.get_barrier_semaphore()
    senders = (core_dev, side_dev, *img_devs, back_dev)
    for device in senders:
        pl.semaphore_signal(barrier, inc=1, device_id=device, device_id_type=MESH)

    @pl.when(last)
    def _():
        pl.semaphore_signal(barrier, inc=1, device_id=z_back, device_id_type=MESH)

    @pl.when(first)
    def _():
        pl.semaphore_signal(barrier, inc=1, device_id=y_back, device_id_type=MESH)
        pl.semaphore_signal(barrier, inc=1, device_id=z_back, device_id_type=MESH)

    for load in loads:
        load.wait()
    prm[c, 0:1, 0:rows] = rowv[0]
    prm[c, 1:2, 0:rows] = rowv[1]
    prm[c, 2:3, 0:rows] = posv[...].astype(F32)
    prm[c, 3:8, 0:rows] = jnp.zeros((5, rows), F32)
    pl.semaphore_wait(barrier, len(senders) + jnp.where(last, 2, jnp.where(first, 1, 0)))

    @pl.when(first)
    def _():
        pl.semaphore_signal(ready, inc=1, device_id=z_next, device_id_type=MESH)

    scale = scale_ref[0, 0]
    base_own = (grp * rows).astype(F32)
    base_side = ((z * 4 + x_b) * rows).astype(F32)
    two = range(PIECES)

    t_side = copy(T_SIDE, tx.at[0, own], tx.at[0, side], side_dev)
    t_next = [copy(T_NEXT + i, tx.at[0, part(i)], tx.at[1, part(i)], next_dev) for i in two]
    t_relay = copy(T_RELAY, tx.at[0, part(PIECES - 1)], relay.at[0], z_next)
    t_passed = copy(T_NEXT + PIECES - 1, relay.at[0], tx.at[1, part(PIECES - 1)], y_next)
    t_hop = [copy(T_HOP + i, tx.at[1, part(i)], tx.at[1, side_part(i)], side_dev) for i in two]
    t_far = [copy(T_FAR + i, tx.at[1, part(i)], tx.at[2, part(i)], next_dev) for i in two]
    t_far_hop = [copy(T_FAR_HOP + i, tx.at[2, part(i)], tx.at[2, side_part(i)], side_dev) for i in two]
    img_a = copy(IMG, img.at[c, own], img.at[c, slot(1)], a_dev)
    img_z = [copy(IMG_Z + i, img.at[c, part(i)], img.at[c, slot_part(2, i)], z_dev) for i in two]
    img_az = [copy(IMG_AZ + i, img.at[c, slot_part(2, i)], img.at[c, slot_part(3, i)], a_dev) for i in two]
    params = [copy(PRM + i, prm.at[c, :, own], prm.at[c, :, slot(i + 1)], img_devs[i]) for i in range(3)]
    img_core = [copy(IMG_CORE + i, img.at[c, slot(i)], img.at[c, slot(i)], core_dev) for i in range(4)]
    prm_core = copy(PRM_CORE, prm.at[c], prm.at[c], core_dev)
    img_got = [copy(IMG_CORE + i, img.at[1 - c, slot(i)], img.at[1 - c, slot(i)], core_dev) for i in range(4)]
    prm_got = copy(PRM_CORE, prm.at[1 - c], prm.at[1 - c], core_dev)

    g_side = copy(G_SIDE, side_out, side_in, side_dev)
    g_hop = [copy(G_HOP + i, hop_out.at[0, part(i)], hop_in.at[0, part(i)], side_dev) for i in two]
    g_far_hop = [copy(G_FAR_HOP + i, hop_out.at[1, part(i)], hop_in.at[1, part(i)], side_dev) for i in two]
    g_back = [copy(G_BACK + i, back_out.at[0, part(i)], back_in.at[0, part(i)], back_dev) for i in two]
    g_relay = copy(G_RELAY, back_out.at[0, part(PIECES - 1)], relay.at[1], z_back)
    g_passed = copy(G_BACK + PIECES - 1, relay.at[1], back_in.at[0, part(PIECES - 1)], y_back)
    g_far = [copy(G_FAR + i, back_out.at[1, part(i)], back_in.at[1, part(i)], back2_dev) for i in two]
    ig_core = [copy(IG_CORE + i, core_out.at[slot(i)], core_in.at[slot(i)], core_dev) for i in range(4)]
    ig_a = copy(IG, img_out.at[0], img_in.at[0], a_dev)
    ig_z = copy(IG + 1, img_out.at[1], img_in.at[1], z_dev)
    ig_az = copy(IG + 2, img_out.at[2], img_in.at[2], a_dev)

    pl.when(last)(t_relay.start)
    for i in two[:-1]:
        t_next[i].start()
    pl.when(jnp.logical_not(last))(t_next[-1].start)
    for i in two:
        img_z[i].start()
    img_a.start()
    for i in range(3):
        params[i].start()
    t_side.start()
    img_core[0].start()

    for i in two:
        if i == PIECES - 1:

            @pl.when(last)
            def _():
                t_relay.wait_recv()
                t_passed.start()

        img_z[i].wait_recv()
        img_az[i].start()
        t_next[i].wait_recv()
        pl.when(c == 1)(t_far[i].start)
        t_hop[i].start()
    img_core[2].start()
    img_a.wait_recv()
    img_core[1].start()
    for i in two:
        img_az[i].wait_recv()
    img_core[3].start()
    for i in range(3):
        params[i].wait_recv()
    prm_core.start()

    @pl.when(c == 1)
    def _():
        for i in two:
            t_far[i].wait_recv()
            t_far_hop[i].start()

    t_side.wait_recv()

    def tile(s, _):
        j = (s + 1) // 2 - (s // 3) * (2 - 2 * c)
        i = c + (s // 2) * (1 - 2 * c)

        @pl.when(s == 1)
        def _():
            for q in two:
                t_hop[q].wait_recv()

        @pl.when(s == 2)
        def _():
            for q in range(4):
                img_got[q].wait_recv()
            prm_got.wait_recv()

        @pl.when((s == 3) & (c == 1))
        def _():
            for q in two:
                t_far_hop[q].wait_recv()

        scores = lax.dot_general(tx[j], img[i], (((1,), (1,)), ((), ())), preferred_element_type=F32)
        prob = jnp.exp(scale * scores - prm[i, 0:1, :])
        row = lax.broadcasted_iota(jnp.int32, scores.shape, 0)
        place = jnp.where(row < rows, row.astype(F32) + base_own, (row - rows).astype(F32) + base_side)
        place = place + (s * 65536).astype(F32)
        prob = prob - jnp.where(place == prm[i, 2:3, :], 1.0, 0.0)
        w[...] = (prob * (scale * prm[i, 1:2, :])).astype(BF16)
        term = jnp.dot(w[...], img[i], preferred_element_type=F32)
        fresh = (s < 2) | ((s == 3) & (c == 1))

        @pl.when(fresh)
        def _():
            tg[j] = term

        @pl.when(jnp.logical_not(fresh))
        def _():
            tg[j] += term

        @pl.when(((s == 0) & (c == 1)) | ((s == 3) & (c == 0)))
        def _():
            side_out[...] = tg[0, side].astype(BF16)
            g_side.start()

        @pl.when(s == 2)
        def _():
            for q in two:
                hop_out[0, part(q)] = tg[1, side_part(q)].astype(BF16)
                g_hop[q].start()

        @pl.when((s == 3) & (c == 1))
        def _():
            for q in two:
                hop_out[1, part(q)] = tg[2, side_part(q)].astype(BF16)
                g_far_hop[q].start()

        back = lax.dot_general(w[...], tx[j], (((0,), (0,)), ((), ())), preferred_element_type=F32)

        @pl.when(s % 2 == 0)
        def _():
            ig[i] = back

        @pl.when(s % 2 == 1)
        def _():
            ig[i] += back

        return 0

    lax.fori_loop(0, 4, tile, 0)

    for i in (3, 1, 2, 0):
        core_out[slot(i)] = ig[1 - c, slot(i)].astype(BF16)
        ig_core[i].start()

    for i, send in ((3, ig_az), (1, ig_a)):
        ig_core[i].wait_recv()
        img_out[i - 1] = (ig[c, slot(i)] + core_in[slot(i)].astype(F32)).astype(BF16)
        send.start()
    ig_core[2].wait_recv()
    ig[c, slot(2)] += core_in[slot(2)].astype(F32)

    for i in two:
        g_hop[i].wait_recv()
        back_out[0, part(i)] = (tg[1, part(i)] + hop_in[0, part(i)].astype(F32)).astype(BF16)
        if i < PIECES - 1:
            g_back[i].start()
        else:
            pl.when(jnp.logical_not(first))(g_back[i].start)

            @pl.when(first)
            def _():
                pl.semaphore_wait(ready, 1)
                g_relay.start()


    @pl.when(c == 1)
    def _():
        for i in two:
            g_far_hop[i].wait_recv()
            back_out[1, part(i)] = (tg[2, part(i)] + hop_in[1, part(i)].astype(F32)).astype(BF16)
            g_far[i].start()

    ig_az.wait_recv()
    img_out[1] = (ig[c, slot(2)] + img_in[2].astype(F32)).astype(BF16)
    ig_z.start()

    @pl.when(first)
    def _():
        g_relay.wait_recv()
        g_passed.start()

    ig_core[0].wait_recv()
    ig[c, own] += core_in[own].astype(F32)
    g_side.wait_recv()
    tg[0, own] += side_in[...].astype(F32)

    ig_a.wait_recv()
    ig_z.wait_recv()
    image_out[...] = ((ig[c, own] + img_in[0].astype(F32)) + img_in[1].astype(F32)).astype(BF16)

    for i in two:
        g_back[i].wait_recv()

    @pl.when(c == 0)
    def _():
        text_out[...] = (tg[0, own] + back_in[0].astype(F32)).astype(BF16)

    @pl.when(c == 1)
    def _():
        for i in two:
            g_far[i].wait_recv()
        text_out[...] = ((tg[0, own] + back_in[0].astype(F32)) + back_in[1].astype(F32)).astype(BF16)

    for sent in (t_side, *t_next, *t_hop, img_a, *img_z, *img_az, *params, *img_core, prm_core, g_side, *g_hop, *g_back,
                 *ig_core, ig_a, ig_z, ig_az):
        sent.wait_send()

    pl.when(last)(t_relay.wait_send)
    pl.when(first)(g_relay.wait_send)

    @pl.when(c == 1)
    def _():
        for sent in (*t_far, *t_far_hop, *g_far_hop, *g_far):
            sent.wait_send()


def solution(mesh):
    n_blk = mesh.shape["blk"]

    def per_device(image_rows, text_rows, log_norm, row_grad, pos_index, logit_scale):
        rows, width = image_rows.shape
        anywhere = pl.BlockSpec(memory_space=pltpu.HBM)
        return pl.pallas_call(
            functools.partial(kernel, n_blk),
            out_shape=(jax.ShapeDtypeStruct((rows, width), BF16),) * 2,
            in_specs=[pl.BlockSpec(memory_space=pltpu.SMEM)] + [anywhere] * 5,
            out_specs=(pl.BlockSpec(memory_space=pltpu.VMEM),) * 2,
            scratch_shapes=[
                pltpu.VMEM((2, 4 * rows, width), BF16),
                pltpu.VMEM((2, 8, 4 * rows), F32),
                pltpu.VMEM((3, 2 * rows, width), BF16),
                pltpu.VMEM((2, 1, rows), F32),
                pltpu.VMEM((1, rows), jnp.int32),
                pltpu.VMEM((2 * rows, 4 * rows), BF16),
                pltpu.VMEM((3, 2 * rows, width), F32),
                pltpu.VMEM((2, 4 * rows, width), F32),
                pltpu.VMEM((4 * rows, width), BF16),
                pltpu.VMEM((4 * rows, width), BF16),
                pltpu.VMEM((rows, width), BF16),
                pltpu.VMEM((rows, width), BF16),
                pltpu.VMEM((2, rows, width), BF16),
                pltpu.VMEM((2, rows, width), BF16),
                pltpu.VMEM((2, rows, width), BF16),
                pltpu.VMEM((2, rows, width), BF16),
                pltpu.VMEM((3, rows, width), BF16),
                pltpu.VMEM((3, rows, width), BF16),
                pltpu.VMEM((2, rows // PIECES, width), BF16),
                pltpu.SemaphoreType.DMA((5,)),
                pltpu.SemaphoreType.DMA((N_COPIES,)),
                pltpu.SemaphoreType.DMA((N_COPIES,)),
                pltpu.SemaphoreType.REGULAR,
            ],
            compiler_params=pltpu.CompilerParams(
                collective_id=0, has_side_effects=True, vmem_limit_bytes=60 * 2**20
            ),
            name="window_loss_grad",
        )(
            logit_scale.reshape(1, 1), image_rows, text_rows, log_norm.reshape(1, rows),
            row_grad.reshape(1, rows), pos_index.reshape(1, rows),
        )

    return jax.shard_map(
        per_device,
        mesh=mesh,
        in_specs=(
            P(("blk", "group"), None),
            P(("blk", "group"), None),
            P(("blk", "group")),
            P(("blk", "group")),
            P(("blk", "group")),
            P(),
        ),
        out_specs=(P(("blk", "group"), None), P(("blk", "group"), None)),
        check_vma=False,
    )
```

```python
import functools

import jax
import jax.numpy as jnp
from jax import lax
from jax.experimental import pallas as pl
from jax.experimental.pallas import tpu as pltpu
from jax.sharding import PartitionSpec as P

MESH = pl.DeviceIdType.MESH
F32 = jnp.float32
BF16 = jnp.bfloat16
PIECES = 4
LATER = PIECES // 2
Y = 8

HALF = PIECES // 2

T_SIDE = 0
T_NEXT = 1
T_HOP = T_NEXT + PIECES
T_FAR = T_HOP + PIECES
T_FAR_HOP = T_FAR + PIECES
IMG = T_FAR_HOP + PIECES
IMG_Z = IMG + PIECES
IMG_AZ = IMG_Z + PIECES
PRM = IMG_AZ + PIECES
IMG_CORE = PRM + 3
PRM_CORE = IMG_CORE + 4
G_SIDE = PRM_CORE + 1
G_HOP = G_SIDE + 1
G_BACK = G_HOP + PIECES
G_FAR_HOP = G_BACK + PIECES
G_FAR = G_FAR_HOP + PIECES
IG_CORE = G_FAR + PIECES
IG_A = IG_CORE + 4
IG_Z = IG_A + PIECES
IG_AZ = IG_Z + PIECES
T_RELAY = IG_AZ + PIECES
G_RELAY = T_RELAY + LATER
T_FAR_Z = G_RELAY + LATER
T_FAR_PASSED = T_FAR_Z + PIECES
G_FAR_Z = T_FAR_PASSED + PIECES
N_COPIES = G_FAR_Z + PIECES


def kernel(n_blk, scale_ref, image_ref, text_ref, log_ref, grad_ref, pos_ref, image_out, text_out,
           img, prm, tx, rowv, posv, tg, ig, core_out, core_in, side_out, side_in, hop_out, hop_in,
           back_out, back_in, img_out, img_in, relay, image_vm, text_vm, load_sem, send_sem, recv_sem, ready):
    rows = image_ref.shape[0]
    piece = rows // PIECES
    blk, grp = lax.axis_index("blk"), lax.axis_index("group")
    c = blk % 2
    pair = blk // 2
    n_pair = n_blk // 2
    z, x = grp // 4, grp % 4
    x_a = x + 1 - 2 * (x % 2)
    x_b = 3 - x

    def at_pair(step):
        return (((pair + step + n_pair) % n_pair) * 2 + c, grp)

    core_dev = (pair * 2 + 1 - c, grp)
    side_dev = (blk, z * 4 + x_b)
    a_dev, z_dev = (blk, z * 4 + x_a), (blk, (1 - z) * 4 + x)
    img_devs = (a_dev, z_dev, (blk, (1 - z) * 4 + x_a))
    next_dev, back_dev = at_pair(1), at_pair(-1)
    back2_dev = at_pair(-2)
    y = pair % Y
    last, first, before, second = y == Y - 1, y == 0, y == Y - 2, y == 1
    crowded = first | last
    lowest = pair < Y
    z_next, z_back = at_pair(Y), at_pair(-Y)
    y_next, y_back = at_pair((y + 1) % Y - y), at_pair((y + Y - 1) % Y - y)
    y_next2, y_back2 = at_pair((y + 2) % Y - y), at_pair((y + Y - 2) % Y - y)

    own, side = pl.ds(0, rows), pl.ds(rows, rows)

    def slot(i):
        return pl.ds(i * rows, rows)

    def part(i):
        return pl.ds(i * piece, piece)

    def slot_part(s, i):
        return pl.ds(s * rows + i * piece, piece)

    def side_part(i):
        return slot_part(1, i)

    def copy(index, src, dst, device):
        return pltpu.make_async_remote_copy(
            src_ref=src, dst_ref=dst, send_sem=send_sem.at[index], recv_sem=recv_sem.at[index],
            device_id=device, device_id_type=MESH,
        )

    loads = [
        pltpu.make_async_copy(text_ref, tx.at[0, own], load_sem.at[0]),
        pltpu.make_async_copy(image_ref, img.at[c, own], load_sem.at[1]),
        pltpu.make_async_copy(log_ref, rowv.at[0], load_sem.at[2]),
        pltpu.make_async_copy(grad_ref, rowv.at[1], load_sem.at[3]),
        pltpu.make_async_copy(pos_ref, posv, load_sem.at[4]),
    ]
    for load in loads:
        load.start()

    barrier = pltpu.get_barrier_semaphore()
    senders = (core_dev, side_dev, *img_devs, back_dev)
    for device in senders:
        pl.semaphore_signal(barrier, inc=1, device_id=device, device_id_type=MESH)

    @pl.when(last | before | first | second)
    def _():
        pl.semaphore_signal(barrier, inc=1, device_id=z_back, device_id_type=MESH)

    @pl.when(first)
    def _():
        pl.semaphore_signal(barrier, inc=1, device_id=y_back, device_id_type=MESH)
        pl.semaphore_signal(barrier, inc=1, device_id=y_back2, device_id_type=MESH)

    for load in loads:
        load.wait()
    prm[c, 0:1, 0:rows] = rowv[0]
    prm[c, 1:2, 0:rows] = rowv[1]
    prm[c, 2:3, 0:rows] = posv[...].astype(F32)
    prm[c, 3:8, 0:rows] = jnp.zeros((5, rows), F32)
    pl.semaphore_wait(barrier, len(senders) + jnp.where(last | before, 2, jnp.where(first | second, 1, 0)))

    @pl.when(first | (second & (c == 1)))
    def _():
        pl.semaphore_signal(ready, inc=1, device_id=z_next, device_id_type=MESH)

    scale = scale_ref[0, 0]
    base_own = (grp * rows).astype(F32)
    base_side = ((z * 4 + x_b) * rows).astype(F32)
    two = range(PIECES)

    t_side = copy(T_SIDE, tx.at[0, own], tx.at[0, side], side_dev)
    t_next = [copy(T_NEXT + i, tx.at[0, part(i)], tx.at[1, part(i)], next_dev) for i in two]
    later = range(PIECES - LATER, PIECES)
    t_relay = {i: copy(T_RELAY + i - later[0], tx.at[0, part(i)], relay.at[0, part(i)], z_next) for i in later}
    t_passed = {i: copy(T_NEXT + i, relay.at[0, part(i)], tx.at[1, part(i)], y_next) for i in later}
    t_far_z = [copy(T_FAR_Z + i, tx.at[0, part(i)], relay.at[0, part(i)], z_next) for i in two]
    t_far_passed = [copy(T_FAR_PASSED + i, relay.at[0, part(i)], tx.at[2, part(i)], y_next2) for i in two]
    t_hop = [copy(T_HOP + i, tx.at[1, part(i)], tx.at[1, side_part(i)], side_dev) for i in two]
    t_far = [copy(T_FAR + i, tx.at[1, part(i)], tx.at[2, part(i)], next_dev) for i in two]
    t_far_hop = [copy(T_FAR_HOP + i, tx.at[2, part(i)], tx.at[2, side_part(i)], side_dev) for i in two]
    img_a = [copy(IMG + i, img.at[c, part(i)], img.at[c, slot_part(1, i)], a_dev) for i in two]
    img_z = [copy(IMG_Z + i, img.at[c, part(i)], img.at[c, slot_part(2, i)], z_dev) for i in two]
    img_az = [
        copy(IMG_AZ + i, img.at[c, slot_part(2, i)], img.at[c, slot_part(3, i)], a_dev) for i in two
    ]
    img_za = [copy(IMG_AZ + i, img.at[c, slot_part(1, i)], img.at[c, slot_part(3, i)], z_dev) for i in two]
    params = [copy(PRM + i, prm.at[c, :, own], prm.at[c, :, slot(i + 1)], img_devs[i]) for i in range(3)]
    img_core = [copy(IMG_CORE + i, img.at[c, slot(i)], img.at[c, slot(i)], core_dev) for i in range(4)]
    prm_core = copy(PRM_CORE, prm.at[c], prm.at[c], core_dev)
    img_got = [copy(IMG_CORE + i, img.at[1 - c, slot(i)], img.at[1 - c, slot(i)], core_dev) for i in range(4)]
    prm_got = copy(PRM_CORE, prm.at[1 - c], prm.at[1 - c], core_dev)

    g_side = copy(G_SIDE, side_out, side_in, side_dev)
    g_hop = [copy(G_HOP + i, hop_out.at[0, part(i)], hop_in.at[0, part(i)], side_dev) for i in two]
    g_far_hop = [copy(G_FAR_HOP + i, hop_out.at[1, part(i)], hop_in.at[1, part(i)], side_dev) for i in two]
    g_back = [copy(G_BACK + i, back_out.at[0, part(i)], back_in.at[0, part(i)], back_dev) for i in two]
    g_relay = {i: copy(G_RELAY + i - later[0], back_out.at[0, part(i)], relay.at[1, part(i)], z_back) for i in later}
    g_passed = {i: copy(G_BACK + i, relay.at[1, part(i)], back_in.at[0, part(i)], y_back) for i in later}
    g_far_z = [copy(G_FAR_Z + i, back_out.at[1, part(i)], relay.at[1, part(i)], z_back) for i in two]
    g_far_passed = [copy(G_FAR + i, relay.at[1, part(i)], back_in.at[1, part(i)], y_back2) for i in two]
    g_far = [copy(G_FAR + i, back_out.at[1, part(i)], back_in.at[1, part(i)], back2_dev) for i in two]
    ig_core = [copy(IG_CORE + i, core_out.at[slot(i)], core_in.at[slot(i)], core_dev) for i in range(4)]
    ig_a = [copy(IG_A + i, img_out.at[0, part(i)], img_in.at[0, part(i)], a_dev) for i in two]
    ig_z = [copy(IG_Z + i, img_out.at[1, part(i)], img_in.at[1, part(i)], z_dev) for i in two]
    ig_az = [
        copy(IG_AZ + i, img_out.at[2, part(i)], img_in.at[2, part(i)], a_dev) for i in two
    ]
    ig_za = [copy(IG_AZ + i, img_out.at[2, part(i)], img_in.at[2, part(i)], z_dev) for i in two]
    free = jnp.logical_not(crowded)

    for i in later:
        pl.when(last)(t_relay[i].start)
    for i in two:
        if i in later:
            pl.when(jnp.logical_not(last))(t_next[i].start)
        else:
            t_next[i].start()
    for i in two:
        pl.when(before & (c == 1))(t_far_z[i].start)
    early, late = two[:HALF], two[HALF:]
    for i, k in zip(early, late):
        img_z[i].start()
        img_a[k].start()
    for i, k in zip(early, late):
        img_z[k].start()
        img_a[i].start()
    for i in range(3):
        params[i].start()
    t_side.start()
    img_core[0].start()
    tg[...] = jnp.zeros_like(tg)
    ig[...] = jnp.zeros_like(ig)

    def pass_relayed():
        for i in later:
            t_relay[i].wait_recv()
            t_passed[i].start()

    def pass_far_relayed():
        for i in two:
            t_far_z[i].wait_recv()
            t_far_passed[i].start()

    def pass_next():
        for i in two:
            if i == later[0]:
                pl.when(last & jnp.logical_not(lowest))(pass_relayed)
            t_next[i].wait_recv()
            pl.when((c == 1) & jnp.logical_not(last))(t_far[i].start)
            t_hop[i].start()
        pl.when(before & jnp.logical_not(lowest) & (c == 1))(pass_far_relayed)

    def pass_far():
        for i in two:
            pl.when(first)(t_far_passed[i].wait_recv)
            pl.when(jnp.logical_not(first))(t_far[i].wait_recv)
            t_far_hop[i].start()

    for i, k in zip(early, late):
        img_z[i].wait_recv()
        img_az[i].start()
        @pl.when(free)
        def _():
            img_a[k].wait_recv()
            img_za[k].start()

        @pl.when(crowded)
        def _():
            img_z[k].wait_recv()
            img_az[k].start()

    pl.when(jnp.logical_not(first))(pass_next)
    for i in early:
        img_a[i].wait_recv()
    pl.when(free)(img_core[1].start)
    for i in late:
        pl.when(crowded)(img_a[i].wait_recv)
    pl.when(crowded)(img_core[1].start)
    for i in late:
        pl.when(free)(img_z[i].wait_recv)
    img_core[2].start()
    for i in two:
        img_az[i].wait_recv()
    img_core[3].start()
    for i in range(3):
        params[i].wait_recv()
    prm_core.start()
    pl.when(first)(pass_next)
    pl.when(first & (c == 1))(pass_far)
    pl.when(last & lowest)(pass_relayed)
    pl.when(before & lowest & (c == 1))(pass_far_relayed)
    t_side.wait_recv()

    def tile(s, _):
        j = (s + 1) // 2 - (s // 3) * (2 - 2 * c)
        other = s // 2
        i = c + other * (1 - 2 * c)

        @pl.when(s == 1)
        def _():
            pl.when((c == 1) & jnp.logical_not(first | second))(pass_far)
            for q in two:
                t_hop[q].wait_recv()

        @pl.when(s == 2)
        def _():
            for q in range(4):
                img_got[q].wait_recv()
            prm_got.wait_recv()

        @pl.when((s == 3) & (c == 1))
        def _():
            pl.when(second)(pass_far)
            for q in two:
                t_far_hop[q].wait_recv()

        scores = lax.dot_general(tx[j], img[i], (((1,), (1,)), ((), ())), preferred_element_type=F32)
        prob = jnp.exp(scale * scores - prm[i, 0:1, :])
        row = lax.broadcasted_iota(jnp.int32, scores.shape, 0)
        place = jnp.where(row < rows, row.astype(F32) + base_own, (row - rows).astype(F32) + base_side)
        place = place + (s * 65536).astype(F32)
        prob = prob - jnp.where(place == prm[i, 2:3, :], 1.0, 0.0)
        weight = (prob * (scale * prm[i, 1:2, :])).astype(BF16)
        tg[j] += jnp.dot(weight, img[i], preferred_element_type=F32)
        ig[i] += lax.dot_general(weight, tx[j], (((0,), (0,)), ((), ())), preferred_element_type=F32)

        @pl.when((s == 0) & (c == 1))
        def _():
            side_out[...] = tg[0, side].astype(BF16)
            g_side.start()

        @pl.when(s == 2)
        def _():
            for q in two:
                hop_out[0, part(q)] = tg[1, side_part(q)].astype(BF16)
                g_hop[q].start()

        @pl.when((s == 3) & (c == 1))
        def _():
            for q in two:
                hop_out[1, part(q)] = tg[2, side_part(q)].astype(BF16)
                g_far_hop[q].start()

        return 0

    lax.fori_loop(0, 4, tile, 0)

    for i in (3, 1, 2, 0):
        core_out[slot(i)] = ig[1 - c, slot(i)].astype(BF16)
        ig_core[i].start()

    def ready_part(n, i):
        return ig[c, slot_part(n, i)] + core_in[slot_part(n, i)].astype(F32)

    ig_core[3].wait_recv()
    for i, k in zip(early, late):
        for q in (i, k):
            img_out[2, part(q)] = ready_part(3, q).astype(BF16)
        ig_az[i].start()
        pl.when(crowded)(ig_az[k].start)
        pl.when(free)(ig_za[k].start)
    ig_core[1].wait_recv()
    ig_core[2].wait_recv()
    for i, k in zip(early, late):
        img_out[0, part(i)] = ready_part(1, i).astype(BF16)
        ig_a[i].start()

        @pl.when(free)
        def _():
            img_out[1, part(k)] = ready_part(2, k).astype(BF16)
            ig_z[k].start()

        @pl.when(crowded)
        def _():
            img_out[0, part(k)] = ready_part(1, k).astype(BF16)
            ig_a[k].start()

    for i in two:
        g_hop[i].wait_recv()
        back_out[0, part(i)] = (tg[1, part(i)] + hop_in[0, part(i)].astype(F32)).astype(BF16)
        if i in later:
            pl.when(jnp.logical_not(first))(g_back[i].start)

            @pl.when(first)
            def _():
                if i == later[0]:
                    pl.semaphore_wait(ready, 1)
                g_relay[i].start()
        else:
            g_back[i].start()

    @pl.when(c == 0)
    def _():
        side_out[...] = tg[0, side].astype(BF16)
        g_side.start()

    def far_back(i):
        @pl.when(c == 1)
        def _():
            g_far_hop[i].wait_recv()
            back_out[1, part(i)] = (tg[2, part(i)] + hop_in[1, part(i)].astype(F32)).astype(BF16)
            pl.when(jnp.logical_not(second))(g_far[i].start)

            @pl.when(second)
            def _():
                if i == 0:
                    pl.semaphore_wait(ready, 1)
                g_far_z[i].start()

    for i, k in zip(early, late):
        far_back(2 * i)
        ig_az[i].wait_recv()
        img_out[1, part(i)] = (ready_part(2, i) + img_in[2, part(i)].astype(F32)).astype(BF16)
        ig_z[i].start()
        far_back(2 * i + 1)
        ig_az[k].wait_recv()

        @pl.when(free)
        def _():
            img_out[0, part(k)] = (ready_part(1, k) + img_in[2, part(k)].astype(F32)).astype(BF16)
            ig_a[k].start()

        @pl.when(crowded)
        def _():
            img_out[1, part(k)] = (ready_part(2, k) + img_in[2, part(k)].astype(F32)).astype(BF16)
            ig_z[k].start()

    @pl.when(first)
    def _():
        for i in later:
            g_relay[i].wait_recv()
            g_passed[i].start()

    @pl.when(second & (c == 1))
    def _():
        for i in two:
            g_far_z[i].wait_recv()
            g_far_passed[i].start()

    ig_core[0].wait_recv()
    ig[c, own] += core_in[own].astype(F32)
    g_side.wait_recv()
    tg[0, own] += side_in[...].astype(F32)

    for i in two:
        ig_a[i].wait_recv()
        ig_z[i].wait_recv()
    image_vm[...] = ((ig[c, own] + img_in[0].astype(F32)) + img_in[1].astype(F32)).astype(BF16)

    image_store = pltpu.make_async_copy(image_vm, image_out, load_sem.at[0])
    image_store.start()
    for i in two:
        g_back[i].wait_recv()

    @pl.when(c == 0)
    def _():
        text_vm[...] = (tg[0, own] + back_in[0].astype(F32)).astype(BF16)

    @pl.when(c == 1)
    def _():
        for i in two:
            g_far[i].wait_recv()
        text_vm[...] = ((tg[0, own] + back_in[0].astype(F32)) + back_in[1].astype(F32)).astype(BF16)

    text_store = pltpu.make_async_copy(text_vm, text_out, load_sem.at[1])
    text_store.start()

    for sent in (t_side, *t_next, *t_hop, *img_a, *img_z, *img_az, *params, *img_core, prm_core, g_side, *g_hop, *g_back,
                 *ig_core, *ig_a, *ig_z, *ig_az):
        sent.wait_send()

    for i in later:
        pl.when(last)(t_relay[i].wait_send)
        pl.when(first)(g_relay[i].wait_send)

    @pl.when(c == 1)
    def _():
        for sent in (*t_far_hop, *g_far_hop, *g_far):
            sent.wait_send()
        for sent in g_far_z:
            pl.when(second)(sent.wait_send)
        for i in two:
            pl.when(jnp.logical_not(last))(t_far[i].wait_send)
            pl.when(before)(t_far_z[i].wait_send)
            pl.when(before)(t_far_passed[i].wait_send)
    image_store.wait()
    text_store.wait()


def hand_over(image_ref, text_ref, image_out, text_out, held, load_sem, store_sem):
    half = image_ref.shape[0] // 2
    pieces = [(n, i) for n in range(2) for i in range(2)]
    loads, stores = [], []
    for n, i in pieces:
        rows = pl.ds(i * half, half)
        source, target = (image_ref, image_out) if n == 0 else (text_ref, text_out)
        k = 2 * n + i
        loads.append(pltpu.make_async_copy(source.at[rows], held.at[k], load_sem.at[k]))
        stores.append(pltpu.make_async_copy(held.at[k], target.at[rows], store_sem.at[k]))
    for load in loads:
        load.start()
    for load, store in zip(loads, stores):
        load.wait()
        store.start()
    for store in stores:
        store.wait()


def solution(mesh):
    n_blk = mesh.shape["blk"]

    def per_device(image_rows, text_rows, log_norm, row_grad, pos_index, logit_scale):
        rows, width = image_rows.shape
        anywhere = pl.BlockSpec(memory_space=pltpu.HBM)
        grads = pl.pallas_call(
            functools.partial(kernel, n_blk),
            out_shape=(jax.ShapeDtypeStruct((rows, width), BF16),) * 2,
            in_specs=[pl.BlockSpec(memory_space=pltpu.SMEM)] + [anywhere] * 5,
            out_specs=(anywhere,) * 2,
            scratch_shapes=[
                pltpu.VMEM((2, 4 * rows, width), BF16),
                pltpu.VMEM((2, 8, 4 * rows), F32),
                pltpu.VMEM((3, 2 * rows, width), BF16),
                pltpu.VMEM((2, 1, rows), F32),
                pltpu.VMEM((1, rows), jnp.int32),
                pltpu.VMEM((3, 2 * rows, width), F32),
                pltpu.VMEM((2, 4 * rows, width), F32),
                pltpu.VMEM((4 * rows, width), BF16),
                pltpu.VMEM((4 * rows, width), BF16),
                pltpu.VMEM((rows, width), BF16),
                pltpu.VMEM((rows, width), BF16),
                pltpu.VMEM((2, rows, width), BF16),
                pltpu.VMEM((2, rows, width), BF16),
                pltpu.VMEM((2, rows, width), BF16),
                pltpu.VMEM((2, rows, width), BF16),
                pltpu.VMEM((3, rows, width), BF16),
                pltpu.VMEM((3, rows, width), BF16),
                pltpu.VMEM((2, rows, width), BF16),
                pltpu.VMEM((rows, width), BF16),
                pltpu.VMEM((rows, width), BF16),
                pltpu.SemaphoreType.DMA((5,)),
                pltpu.SemaphoreType.DMA((N_COPIES,)),
                pltpu.SemaphoreType.DMA((N_COPIES,)),
                pltpu.SemaphoreType.REGULAR,
            ],
            compiler_params=pltpu.CompilerParams(
                collective_id=0, has_side_effects=True, vmem_limit_bytes=60 * 2**20
            ),
            name="window_loss_grad",
        )(
            logit_scale.reshape(1, 1), image_rows, text_rows, log_norm.reshape(1, rows),
            row_grad.reshape(1, rows), pos_index.reshape(1, rows),
        )
        return pl.pallas_call(
            hand_over,
            out_shape=(jax.ShapeDtypeStruct((rows, width), BF16),) * 2,
            in_specs=[anywhere] * 2,
            out_specs=(anywhere,) * 2,
            scratch_shapes=[
                pltpu.VMEM((4, rows // 2, width), BF16),
                pltpu.SemaphoreType.DMA((4,)),
                pltpu.SemaphoreType.DMA((4,)),
            ],
            compiler_params=pltpu.CompilerParams(vmem_limit_bytes=60 * 2**20),
            name="hand_over",
        )(*grads)

    return jax.shard_map(
        per_device,
        mesh=mesh,
        in_specs=(
            P(("blk", "group"), None),
            P(("blk", "group"), None),
            P(("blk", "group")),
            P(("blk", "group")),
            P(("blk", "group")),
            P(),
        ),
        out_specs=(P(("blk", "group"), None), P(("blk", "group"), None)),
        check_vma=False,
    )
```

```python
import functools

import jax
import jax.numpy as jnp
from jax import lax
from jax.experimental import pallas as pl
from jax.experimental.pallas import tpu as pltpu
from jax.sharding import PartitionSpec as P

MESH = pl.DeviceIdType.MESH
F32 = jnp.float32
BF16 = jnp.bfloat16
PIECES = 4
LATER = 2
BACK_LATER = 1
Y = 8

HALF = PIECES // 2

T_SIDE = 0
T_NEXT = 1
T_HOP = T_NEXT + PIECES
T_FAR = T_HOP + PIECES
T_FAR_HOP = T_FAR + PIECES
IMG = T_FAR_HOP + PIECES
IMG_Z = IMG + PIECES
IMG_AZ = IMG_Z + PIECES
PRM = IMG_AZ + PIECES
IMG_CORE = PRM + 3
PRM_CORE = IMG_CORE + 4
G_SIDE = PRM_CORE + 1
G_HOP = G_SIDE + 1
G_BACK = G_HOP + PIECES
G_FAR_HOP = G_BACK + PIECES
G_FAR = G_FAR_HOP + PIECES
IG_CORE = G_FAR + PIECES
IG_A = IG_CORE + 4
IG_Z = IG_A + PIECES
IG_AZ = IG_Z + PIECES
T_RELAY = IG_AZ + PIECES
G_RELAY = T_RELAY + LATER
T_FAR_Z = G_RELAY + BACK_LATER
T_FAR_PASSED = T_FAR_Z + PIECES
G_FAR_Z = T_FAR_PASSED + PIECES
N_COPIES = G_FAR_Z + PIECES


def kernel(n_blk, scale_ref, image_ref, text_ref, log_ref, grad_ref, pos_ref, image_out, text_out,
           img, prm, tx, rowv, posv, tg, ig, core_out, core_in, side_out, side_in, hop_out, hop_in,
           back_out, back_in, img_out, img_in, relay, image_vm, text_vm, load_sem, send_sem, recv_sem, ready):
    rows = image_ref.shape[0]
    piece = rows // PIECES
    blk, grp = lax.axis_index("blk"), lax.axis_index("group")
    c = blk % 2
    pair = blk // 2
    n_pair = n_blk // 2
    z, x = grp // 4, grp % 4
    x_a = x + 1 - 2 * (x % 2)
    x_b = 3 - x

    def at_pair(step):
        return (((pair + step + n_pair) % n_pair) * 2 + c, grp)

    core_dev = (pair * 2 + 1 - c, grp)
    side_dev = (blk, z * 4 + x_b)
    a_dev, z_dev = (blk, z * 4 + x_a), (blk, (1 - z) * 4 + x)
    img_devs = (a_dev, z_dev, (blk, (1 - z) * 4 + x_a))
    next_dev, back_dev = at_pair(1), at_pair(-1)
    back2_dev = at_pair(-2)
    y = pair % Y
    last, first, before, second = y == Y - 1, y == 0, y == Y - 2, y == 1
    crowded = first | last
    lowest = pair < Y
    z_next, z_back = at_pair(Y), at_pair(-Y)
    y_next, y_back = at_pair((y + 1) % Y - y), at_pair((y + Y - 1) % Y - y)
    y_next2, y_back2 = at_pair((y + 2) % Y - y), at_pair((y + Y - 2) % Y - y)

    own, side = pl.ds(0, rows), pl.ds(rows, rows)

    def slot(i):
        return pl.ds(i * rows, rows)

    def part(i):
        return pl.ds(i * piece, piece)

    def slot_part(s, i):
        return pl.ds(s * rows + i * piece, piece)

    def side_part(i):
        return slot_part(1, i)

    def copy(index, src, dst, device):
        return pltpu.make_async_remote_copy(
            src_ref=src, dst_ref=dst, send_sem=send_sem.at[index], recv_sem=recv_sem.at[index],
            device_id=device, device_id_type=MESH,
        )

    loads = [
        pltpu.make_async_copy(text_ref, tx.at[0, own], load_sem.at[0]),
        pltpu.make_async_copy(image_ref, img.at[c, own], load_sem.at[1]),
        pltpu.make_async_copy(log_ref, rowv.at[0], load_sem.at[2]),
        pltpu.make_async_copy(grad_ref, rowv.at[1], load_sem.at[3]),
        pltpu.make_async_copy(pos_ref, posv, load_sem.at[4]),
    ]
    barrier = pltpu.get_barrier_semaphore()
    senders = (core_dev, side_dev, *img_devs, back_dev)
    for device in senders:
        pl.semaphore_signal(barrier, inc=1, device_id=device, device_id_type=MESH)

    @pl.when(last | before | first | second)
    def _():
        pl.semaphore_signal(barrier, inc=1, device_id=z_back, device_id_type=MESH)

    @pl.when(first)
    def _():
        pl.semaphore_signal(barrier, inc=1, device_id=y_back, device_id_type=MESH)
        pl.semaphore_signal(barrier, inc=1, device_id=y_back2, device_id_type=MESH)

    for load in loads:
        load.start()
    for load in loads:
        load.wait()
    prm[c, 0:1, 0:rows] = rowv[0]
    prm[c, 1:2, 0:rows] = rowv[1]
    prm[c, 2:3, 0:rows] = posv[...].astype(F32)
    prm[c, 3:8, 0:rows] = jnp.zeros((5, rows), F32)
    pl.semaphore_wait(barrier, len(senders) + jnp.where(last | before, 2, jnp.where(first | second, 1, 0)))

    @pl.when(first | (second & (c == 1)))
    def _():
        pl.semaphore_signal(ready, inc=1, device_id=z_next, device_id_type=MESH)

    scale = scale_ref[0, 0]
    base_own = (grp * rows).astype(F32)
    base_side = ((z * 4 + x_b) * rows).astype(F32)
    two = range(PIECES)

    t_side = copy(T_SIDE, tx.at[0, own], tx.at[0, side], side_dev)
    t_next = [copy(T_NEXT + i, tx.at[0, part(i)], tx.at[1, part(i)], next_dev) for i in two]
    later = range(PIECES - LATER, PIECES)
    by_z = {i: last & ((z == 1) | (i == later[-1])) for i in later}
    back_later = range(PIECES - BACK_LATER, PIECES)
    t_relay = {i: copy(T_RELAY + i - later[0], tx.at[0, part(i)], relay.at[0, part(i)], z_next) for i in later}
    t_passed = {i: copy(T_NEXT + i, relay.at[0, part(i)], tx.at[1, part(i)], y_next) for i in later}
    t_far_z = [copy(T_FAR_Z + i, tx.at[0, part(i)], relay.at[0, part(i)], z_next) for i in two]
    t_far_passed = [copy(T_FAR_PASSED + i, relay.at[0, part(i)], tx.at[2, part(i)], y_next2) for i in two]
    t_hop = [copy(T_HOP + i, tx.at[1, part(i)], tx.at[1, side_part(i)], side_dev) for i in two]
    t_far = [copy(T_FAR + i, tx.at[1, part(i)], tx.at[2, part(i)], next_dev) for i in two]
    t_far_hop = [copy(T_FAR_HOP + i, tx.at[2, part(i)], tx.at[2, side_part(i)], side_dev) for i in two]
    img_a = [copy(IMG + i, img.at[c, part(i)], img.at[c, slot_part(1, i)], a_dev) for i in two]
    img_z = [copy(IMG_Z + i, img.at[c, part(i)], img.at[c, slot_part(2, i)], z_dev) for i in two]
    img_az = [
        copy(IMG_AZ + i, img.at[c, slot_part(2, i)], img.at[c, slot_part(3, i)], a_dev) for i in two
    ]
    img_za = [copy(IMG_AZ + i, img.at[c, slot_part(1, i)], img.at[c, slot_part(3, i)], z_dev) for i in two]
    params = [copy(PRM + i, prm.at[c, :, own], prm.at[c, :, slot(i + 1)], img_devs[i]) for i in range(3)]
    img_core = [copy(IMG_CORE + i, img.at[c, slot(i)], img.at[c, slot(i)], core_dev) for i in range(4)]
    prm_core = copy(PRM_CORE, prm.at[c], prm.at[c], core_dev)
    img_got = [copy(IMG_CORE + i, img.at[1 - c, slot(i)], img.at[1 - c, slot(i)], core_dev) for i in range(4)]
    prm_got = copy(PRM_CORE, prm.at[1 - c], prm.at[1 - c], core_dev)

    g_side = copy(G_SIDE, side_out, side_in, side_dev)
    g_hop = [copy(G_HOP + i, hop_out.at[0, part(i)], hop_in.at[0, part(i)], side_dev) for i in two]
    g_far_hop = [copy(G_FAR_HOP + i, hop_out.at[1, part(i)], hop_in.at[1, part(i)], side_dev) for i in two]
    g_back = [copy(G_BACK + i, back_out.at[0, part(i)], back_in.at[0, part(i)], back_dev) for i in two]
    g_relay = {i: copy(G_RELAY + i - back_later[0], back_out.at[0, part(i)], relay.at[1, part(i)], z_back) for i in back_later}
    g_passed = {i: copy(G_BACK + i, relay.at[1, part(i)], back_in.at[0, part(i)], y_back) for i in back_later}
    g_far_z = [copy(G_FAR_Z + i, back_out.at[1, part(i)], relay.at[1, part(i)], z_back) for i in two]
    g_far_passed = [copy(G_FAR + i, relay.at[1, part(i)], back_in.at[1, part(i)], y_back2) for i in two]
    g_far = [copy(G_FAR + i, back_out.at[1, part(i)], back_in.at[1, part(i)], back2_dev) for i in two]
    ig_core = [copy(IG_CORE + i, core_out.at[slot(i)], core_in.at[slot(i)], core_dev) for i in range(4)]
    ig_a = [copy(IG_A + i, img_out.at[0, part(i)], img_in.at[0, part(i)], a_dev) for i in two]
    ig_z = [copy(IG_Z + i, img_out.at[1, part(i)], img_in.at[1, part(i)], z_dev) for i in two]
    ig_az = [
        copy(IG_AZ + i, img_out.at[2, part(i)], img_in.at[2, part(i)], a_dev) for i in two
    ]
    ig_za = [copy(IG_AZ + i, img_out.at[2, part(i)], img_in.at[2, part(i)], z_dev) for i in two]
    free = jnp.logical_not(crowded)

    for i in later:
        pl.when(by_z[i])(t_relay[i].start)
    for i in two:
        if i in later:
            pl.when(jnp.logical_not(by_z[i]))(t_next[i].start)
        else:
            t_next[i].start()
    for i in two:
        pl.when(before & (c == 1))(t_far_z[i].start)
    early, late = two[:HALF], two[HALF:]
    for i, k in zip(early, late):
        img_z[i].start()
        img_a[k].start()
    for i, k in zip(early, late):
        img_z[k].start()
        img_a[i].start()
    for i in range(3):
        params[i].start()
    t_side.start()
    img_core[0].start()
    tg[...] = jnp.zeros_like(tg)
    ig[...] = jnp.zeros_like(ig)

    def pass_relayed():
        for i in later:

            @pl.when(by_z[i])
            def _():
                t_relay[i].wait_recv()
                t_passed[i].start()


    def pass_far_relayed():
        for i in two:
            t_far_z[i].wait_recv()
            t_far_passed[i].start()

    def pass_next():
        for i in two:
            if i == later[0]:
                pl.when(last & jnp.logical_not(lowest))(pass_relayed)
            t_next[i].wait_recv()
            pl.when((c == 1) & jnp.logical_not(last))(t_far[i].start)
            t_hop[i].start()
        pl.when(before & jnp.logical_not(lowest) & (c == 1))(pass_far_relayed)

    def pass_far():
        for i in two:
            pl.when(first)(t_far_passed[i].wait_recv)
            pl.when(jnp.logical_not(first))(t_far[i].wait_recv)
            t_far_hop[i].start()

    for i, k in zip(early, late):
        img_z[i].wait_recv()
        img_az[i].start()
        @pl.when(free)
        def _():
            img_a[k].wait_recv()
            img_za[k].start()

        @pl.when(crowded)
        def _():
            img_z[k].wait_recv()
            img_az[k].start()

    pl.when(jnp.logical_not(first))(pass_next)
    for i in early:
        img_a[i].wait_recv()
    pl.when(free)(img_core[1].start)
    for i in late:
        pl.when(crowded)(img_a[i].wait_recv)
    pl.when(crowded)(img_core[1].start)
    for i in late:
        pl.when(free)(img_z[i].wait_recv)
    img_core[2].start()
    for i in two:
        img_az[i].wait_recv()
    img_core[3].start()
    for i in range(3):
        params[i].wait_recv()
    prm_core.start()
    pl.when(first)(pass_next)
    pl.when(last & lowest)(pass_relayed)
    pl.when(before & lowest & (c == 1))(pass_far_relayed)
    t_side.wait_recv()

    def tile(s, _):
        j = (s + 1) // 2 - (s // 3) * (2 - 2 * c)
        other = s // 2
        i = c + other * (1 - 2 * c)

        @pl.when(s == 1)
        def _():
            pl.when((c == 1) & jnp.logical_not(first | second))(pass_far)
            for q in two:
                t_hop[q].wait_recv()

        @pl.when(s == 2)
        def _():
            for q in range(4):
                img_got[q].wait_recv()
            prm_got.wait_recv()

        @pl.when((s == 2) & (c == 1) & first)
        def _():
            pass_far()

        @pl.when((s == 3) & (c == 1))
        def _():
            pl.when(second)(pass_far)
            for q in two:
                t_far_hop[q].wait_recv()

        scores = lax.dot_general(tx[j], img[i], (((1,), (1,)), ((), ())), preferred_element_type=F32)
        prob = jnp.exp(scale * scores - prm[i, 0:1, :])
        row = lax.broadcasted_iota(jnp.int32, scores.shape, 0)
        place = jnp.where(row < rows, row.astype(F32) + base_own, (row - rows).astype(F32) + base_side)
        place = place + (s * 65536).astype(F32)
        prob = prob - jnp.where(place == prm[i, 2:3, :], 1.0, 0.0)
        weight = (prob * (scale * prm[i, 1:2, :])).astype(BF16)
        tg[j] += jnp.dot(weight, img[i], preferred_element_type=F32)
        ig[i] += lax.dot_general(weight, tx[j], (((0,), (0,)), ((), ())), preferred_element_type=F32)

        @pl.when((s == 0) & (c == 1))
        def _():
            side_out[...] = tg[0, side].astype(BF16)
            g_side.start()

        @pl.when(s == 2)
        def _():
            for q in two:
                hop_out[0, part(q)] = tg[1, side_part(q)].astype(BF16)
                g_hop[q].start()

        @pl.when((s == 3) & (c == 1))
        def _():
            for q in two:
                hop_out[1, part(q)] = tg[2, side_part(q)].astype(BF16)
                g_far_hop[q].start()

        return 0

    lax.fori_loop(0, 4, tile, 0)

    for i in (3, 1, 2, 0):
        core_out[slot(i)] = ig[1 - c, slot(i)].astype(BF16)
        ig_core[i].start()

    def ready_part(n, i):
        return ig[c, slot_part(n, i)] + core_in[slot_part(n, i)].astype(F32)

    ig_core[3].wait_recv()
    for i, k in zip(early, late):
        for q in (i, k):
            img_out[2, part(q)] = ready_part(3, q).astype(BF16)
        ig_az[i].start()
        pl.when(crowded)(ig_az[k].start)
        pl.when(free)(ig_za[k].start)
    ig_core[1].wait_recv()
    ig_core[2].wait_recv()
    for i, k in zip(early, late):
        img_out[0, part(i)] = ready_part(1, i).astype(BF16)
        ig_a[i].start()

        @pl.when(free)
        def _():
            img_out[1, part(k)] = ready_part(2, k).astype(BF16)
            ig_z[k].start()

        @pl.when(crowded)
        def _():
            img_out[0, part(k)] = ready_part(1, k).astype(BF16)
            ig_a[k].start()

    for i in two:
        g_hop[i].wait_recv()
        back_out[0, part(i)] = (tg[1, part(i)] + hop_in[0, part(i)].astype(F32)).astype(BF16)
        if i in back_later:
            pl.when(jnp.logical_not(first))(g_back[i].start)

            @pl.when(first)
            def _():
                if i == back_later[0]:
                    pl.semaphore_wait(ready, 1)
                g_relay[i].start()
        else:
            g_back[i].start()

    @pl.when(c == 0)
    def _():
        side_out[...] = tg[0, side].astype(BF16)
        g_side.start()

    def far_back(i):
        @pl.when(c == 1)
        def _():
            g_far_hop[i].wait_recv()
            back_out[1, part(i)] = (tg[2, part(i)] + hop_in[1, part(i)].astype(F32)).astype(BF16)
            pl.when(jnp.logical_not(second))(g_far[i].start)

            @pl.when(second)
            def _():
                if i == 0:
                    pl.semaphore_wait(ready, 1)
                g_far_z[i].start()

    for i, k in zip(early, late):
        far_back(2 * i)
        ig_az[i].wait_recv()
        img_out[1, part(i)] = (ready_part(2, i) + img_in[2, part(i)].astype(F32)).astype(BF16)
        ig_z[i].start()
        far_back(2 * i + 1)
        ig_az[k].wait_recv()

        @pl.when(free)
        def _():
            img_out[0, part(k)] = (ready_part(1, k) + img_in[2, part(k)].astype(F32)).astype(BF16)
            ig_a[k].start()

        @pl.when(crowded)
        def _():
            img_out[1, part(k)] = (ready_part(2, k) + img_in[2, part(k)].astype(F32)).astype(BF16)
            ig_z[k].start()

    for sent in (t_side, *t_next, *t_hop, *img_a, *img_z, *img_az, *params, *img_core, prm_core, g_side, *g_hop, *ig_core):
        sent.wait_send()
    for i in later:
        pl.when(by_z[i])(t_relay[i].wait_send)

    @pl.when(c == 1)
    def _():
        for sent in (*t_far_hop, *g_far_hop):
            sent.wait_send()
        for i in two:
            pl.when(jnp.logical_not(last))(t_far[i].wait_send)
            pl.when(before)(t_far_z[i].wait_send)
            pl.when(before)(t_far_passed[i].wait_send)

    @pl.when(first)
    def _():
        for i in back_later:
            g_relay[i].wait_recv()
            g_passed[i].start()

    @pl.when(second & (c == 1))
    def _():
        for i in two:
            g_far_z[i].wait_recv()
            g_far_passed[i].start()

    ig_core[0].wait_recv()
    ig[c, own] += core_in[own].astype(F32)
    g_side.wait_recv()
    tg[0, own] += side_in[...].astype(F32)

    for i in two:
        ig_a[i].wait_recv()
        ig_z[i].wait_recv()
    image_vm[...] = ((ig[c, own] + img_in[0].astype(F32)) + img_in[1].astype(F32)).astype(BF16)

    image_store = pltpu.make_async_copy(image_vm, image_out, load_sem.at[0])
    image_store.start()
    for sent in (*g_back, *ig_a, *ig_z, *ig_az):
        sent.wait_send()
    for i in back_later:
        pl.when(first)(g_relay[i].wait_send)

    @pl.when(c == 1)
    def _():
        for sent in g_far:
            sent.wait_send()
        for sent in g_far_z:
            pl.when(second)(sent.wait_send)

    for i in two:
        g_back[i].wait_recv()

    @pl.when(c == 0)
    def _():
        text_vm[...] = (tg[0, own] + back_in[0].astype(F32)).astype(BF16)

    @pl.when(c == 1)
    def _():
        for i in two:
            g_far[i].wait_recv()
        text_vm[...] = ((tg[0, own] + back_in[0].astype(F32)) + back_in[1].astype(F32)).astype(BF16)

    text_store = pltpu.make_async_copy(text_vm, text_out, load_sem.at[1])
    text_store.start()

    image_store.wait()
    text_store.wait()


def hand_over(image_ref, text_ref, image_out, text_out, held, load_sem, store_sem):
    half = image_ref.shape[0] // 2
    pieces = [(n, i) for n in range(2) for i in range(2)]
    loads, stores = [], []
    for n, i in pieces:
        rows = pl.ds(i * half, half)
        source, target = (image_ref, image_out) if n == 0 else (text_ref, text_out)
        k = 2 * n + i
        loads.append(pltpu.make_async_copy(source.at[rows], held.at[k], load_sem.at[k]))
        stores.append(pltpu.make_async_copy(held.at[k], target.at[rows], store_sem.at[k]))
    for load in loads:
        load.start()
    for load, store in zip(loads, stores):
        load.wait()
        store.start()
    for store in stores:
        store.wait()


def solution(mesh):
    n_blk = mesh.shape["blk"]

    def per_device(image_rows, text_rows, log_norm, row_grad, pos_index, logit_scale):
        rows, width = image_rows.shape
        anywhere = pl.BlockSpec(memory_space=pltpu.HBM)
        grads = pl.pallas_call(
            functools.partial(kernel, n_blk),
            out_shape=(jax.ShapeDtypeStruct((rows, width), BF16),) * 2,
            in_specs=[pl.BlockSpec(memory_space=pltpu.SMEM)] + [anywhere] * 5,
            out_specs=(anywhere,) * 2,
            scratch_shapes=[
                pltpu.VMEM((2, 4 * rows, width), BF16),
                pltpu.VMEM((2, 8, 4 * rows), F32),
                pltpu.VMEM((3, 2 * rows, width), BF16),
                pltpu.VMEM((2, 1, rows), F32),
                pltpu.VMEM((1, rows), jnp.int32),
                pltpu.VMEM((3, 2 * rows, width), F32),
                pltpu.VMEM((2, 4 * rows, width), F32),
                pltpu.VMEM((4 * rows, width), BF16),
                pltpu.VMEM((4 * rows, width), BF16),
                pltpu.VMEM((rows, width), BF16),
                pltpu.VMEM((rows, width), BF16),
                pltpu.VMEM((2, rows, width), BF16),
                pltpu.VMEM((2, rows, width), BF16),
                pltpu.VMEM((2, rows, width), BF16),
                pltpu.VMEM((2, rows, width), BF16),
                pltpu.VMEM((3, rows, width), BF16),
                pltpu.VMEM((3, rows, width), BF16),
                pltpu.VMEM((2, rows, width), BF16),
                pltpu.VMEM((rows, width), BF16),
                pltpu.VMEM((rows, width), BF16),
                pltpu.SemaphoreType.DMA((5,)),
                pltpu.SemaphoreType.DMA((N_COPIES,)),
                pltpu.SemaphoreType.DMA((N_COPIES,)),
                pltpu.SemaphoreType.REGULAR,
            ],
            compiler_params=pltpu.CompilerParams(
                collective_id=0, has_side_effects=True, vmem_limit_bytes=60 * 2**20
            ),
            name="window_loss_grad",
        )(
            logit_scale.reshape(1, 1), image_rows, text_rows, log_norm.reshape(1, rows),
            row_grad.reshape(1, rows), pos_index.reshape(1, rows),
        )
        return pl.pallas_call(
            hand_over,
            out_shape=(jax.ShapeDtypeStruct((rows, width), BF16),) * 2,
            in_specs=[anywhere] * 2,
            out_specs=(anywhere,) * 2,
            scratch_shapes=[
                pltpu.VMEM((4, rows // 2, width), BF16),
                pltpu.SemaphoreType.DMA((4,)),
                pltpu.SemaphoreType.DMA((4,)),
            ],
            compiler_params=pltpu.CompilerParams(vmem_limit_bytes=60 * 2**20),
            name="hand_over",
        )(*grads)

    return jax.shard_map(
        per_device,
        mesh=mesh,
        in_specs=(
            P(("blk", "group"), None),
            P(("blk", "group"), None),
            P(("blk", "group")),
            P(("blk", "group")),
            P(("blk", "group")),
            P(),
        ),
        out_specs=(P(("blk", "group"), None), P(("blk", "group"), None)),
        check_vma=False,
    )
```

```python
import functools

import jax
import jax.numpy as jnp
from jax import lax
from jax.experimental import pallas as pl
from jax.experimental.pallas import tpu as pltpu
from jax.sharding import PartitionSpec as P

MESH = pl.DeviceIdType.MESH
F32 = jnp.float32
BF16 = jnp.bfloat16
PIECES = 4
LATER = 2
BACK_LATER = 1
Y = 8

HALF = PIECES // 2

T_SIDE = 0
T_NEXT = 1
T_HOP = T_NEXT + PIECES
T_FAR = T_HOP + PIECES
T_FAR_HOP = T_FAR + PIECES
IMG = T_FAR_HOP + PIECES
IMG_Z = IMG + PIECES
IMG_AZ = IMG_Z + PIECES
PRM = IMG_AZ + PIECES
IMG_CORE = PRM + 3
PRM_CORE = IMG_CORE + 4
G_SIDE = PRM_CORE + 1
G_HOP = G_SIDE + 1
G_BACK = G_HOP + PIECES
G_FAR_HOP = G_BACK + PIECES
G_FAR = G_FAR_HOP + PIECES
IG_CORE = G_FAR + PIECES
IG_A = IG_CORE + 4
IG_Z = IG_A + PIECES
IG_AZ = IG_Z + PIECES
T_RELAY = IG_AZ + PIECES
G_RELAY = T_RELAY + LATER
T_FAR_Z = G_RELAY + BACK_LATER
T_FAR_PASSED = T_FAR_Z + PIECES
G_FAR_Z = T_FAR_PASSED + PIECES
T_DIRECT = G_FAR_Z + PIECES
T_PASSED = T_DIRECT + PIECES
N_COPIES = T_PASSED


def kernel(n_blk, scale_ref, image_ref, text_ref, log_ref, grad_ref, pos_ref, image_out, text_out,
           img, prm, tx, rowv, posv, tg, ig, core_out, core_in, side_out, side_in, hop_out, hop_in,
           back_out, back_in, img_out, img_in, relay, image_vm, text_vm, load_sem, send_sem, recv_sem, ready):
    rows = image_ref.shape[0]
    piece = rows // PIECES
    blk, grp = lax.axis_index("blk"), lax.axis_index("group")
    c = blk % 2
    pair = blk // 2
    n_pair = n_blk // 2
    z, x = grp // 4, grp % 4
    x_a = x + 1 - 2 * (x % 2)
    x_b = 3 - x

    def at_pair(step):
        return (((pair + step + n_pair) % n_pair) * 2 + c, grp)

    core_dev = (pair * 2 + 1 - c, grp)
    side_dev = (blk, z * 4 + x_b)
    a_dev, z_dev = (blk, z * 4 + x_a), (blk, (1 - z) * 4 + x)
    img_devs = (a_dev, z_dev, (blk, (1 - z) * 4 + x_a))
    next_dev, back_dev = at_pair(1), at_pair(-1)
    next2_dev, back2_dev = at_pair(2), at_pair(-2)
    y = pair % Y
    last, first, before, second = y == Y - 1, y == 0, y == Y - 2, y == 1
    crowded = first
    lowest = pair < Y
    z_next, z_back = at_pair(Y), at_pair(-Y)
    y_next, y_back = at_pair((y + 1) % Y - y), at_pair((y + Y - 1) % Y - y)
    y_next2, y_back2 = at_pair((y + 2) % Y - y), at_pair((y + Y - 2) % Y - y)

    own, side = pl.ds(0, rows), pl.ds(rows, rows)

    def slot(i):
        return pl.ds(i * rows, rows)

    def part(i):
        return pl.ds(i * piece, piece)

    def slot_part(s, i):
        return pl.ds(s * rows + i * piece, piece)

    def side_part(i):
        return slot_part(1, i)

    def copy(index, src, dst, device):
        return pltpu.make_async_remote_copy(
            src_ref=src, dst_ref=dst, send_sem=send_sem.at[index], recv_sem=recv_sem.at[index],
            device_id=device, device_id_type=MESH,
        )

    loads = [
        pltpu.make_async_copy(text_ref, tx.at[0, own], load_sem.at[0]),
        pltpu.make_async_copy(image_ref, img.at[c, own], load_sem.at[1]),
        pltpu.make_async_copy(log_ref, rowv.at[0], load_sem.at[2]),
        pltpu.make_async_copy(grad_ref, rowv.at[1], load_sem.at[3]),
        pltpu.make_async_copy(pos_ref, posv, load_sem.at[4]),
    ]
    barrier = pltpu.get_barrier_semaphore()
    senders = (core_dev, side_dev, *img_devs, back_dev)
    for device in senders:
        pl.semaphore_signal(barrier, inc=1, device_id=device, device_id_type=MESH)

    @pl.when(last | before | first | second)
    def _():
        pl.semaphore_signal(barrier, inc=1, device_id=z_back, device_id_type=MESH)

    @pl.when(first)
    def _():
        pl.semaphore_signal(barrier, inc=1, device_id=y_back, device_id_type=MESH)
        pl.semaphore_signal(barrier, inc=1, device_id=y_back2, device_id_type=MESH)

    @pl.when(second)
    def _():
        pl.semaphore_signal(barrier, inc=1, device_id=back2_dev, device_id_type=MESH)

    for load in loads:
        load.start()
    for load in loads:
        load.wait()
    prm[c, 0:1, 0:rows] = rowv[0]
    prm[c, 1:2, 0:rows] = rowv[1]
    prm[c, 2:3, 0:rows] = posv[...].astype(F32)
    prm[c, 3:8, 0:rows] = jnp.zeros((5, rows), F32)
    pl.semaphore_wait(barrier, len(senders) + jnp.where(last, 3, jnp.where(before, 2, jnp.where(first | second, 1, 0))))

    @pl.when(first | (second & (c == 1)))
    def _():
        pl.semaphore_signal(ready, inc=1, device_id=z_next, device_id_type=MESH)

    scale = scale_ref[0, 0]
    base_own = (grp * rows).astype(F32)
    base_side = ((z * 4 + x_b) * rows).astype(F32)
    two = range(PIECES)

    t_side = copy(T_SIDE, tx.at[0, own], tx.at[0, side], side_dev)
    t_next = [copy(T_NEXT + i, tx.at[0, part(i)], tx.at[1, part(i)], next_dev) for i in two]
    later = range(PIECES - LATER, PIECES)
    by_z = {i: last & ((z == 1) | (i == later[-1])) for i in later}
    back_later = range(BACK_LATER)
    t_relay = {i: copy(T_RELAY + i - later[0], tx.at[0, part(i)], relay.at[0, part(i)], z_next) for i in later}
    t_passed = {i: copy(T_NEXT + i, relay.at[0, part(i)], tx.at[1, part(i)], y_next) for i in later}
    t_far_z = [copy(T_FAR_Z + i, tx.at[0, part(i)], relay.at[0, part(i)], z_next) for i in two]
    t_far_passed = [copy(T_FAR_PASSED + i, relay.at[0, part(i)], tx.at[2, part(i)], y_next2) for i in two]
    t_direct = [copy(T_DIRECT + i, tx.at[0, part(i)], tx.at[2, part(i)], next2_dev) for i in two]
    t_hop = [copy(T_HOP + i, tx.at[1, part(i)], tx.at[1, side_part(i)], side_dev) for i in two]
    t_far = [copy(T_FAR + i, tx.at[1, part(i)], tx.at[2, part(i)], next_dev) for i in two]
    t_far_hop = [copy(T_FAR_HOP + i, tx.at[2, part(i)], tx.at[2, side_part(i)], side_dev) for i in two]
    img_a = [copy(IMG + i, img.at[c, part(i)], img.at[c, slot_part(1, i)], a_dev) for i in two]
    img_z = [copy(IMG_Z + i, img.at[c, part(i)], img.at[c, slot_part(2, i)], z_dev) for i in two]
    img_az = [
        copy(IMG_AZ + i, img.at[c, slot_part(2, i)], img.at[c, slot_part(3, i)], a_dev) for i in two
    ]
    img_za = [copy(IMG_AZ + i, img.at[c, slot_part(1, i)], img.at[c, slot_part(3, i)], z_dev) for i in two]
    params = [copy(PRM + i, prm.at[c, :, own], prm.at[c, :, slot(i + 1)], img_devs[i]) for i in range(3)]
    img_core = [copy(IMG_CORE + i, img.at[c, slot(i)], img.at[c, slot(i)], core_dev) for i in range(4)]
    prm_core = copy(PRM_CORE, prm.at[c], prm.at[c], core_dev)
    img_got = [copy(IMG_CORE + i, img.at[1 - c, slot(i)], img.at[1 - c, slot(i)], core_dev) for i in range(4)]
    prm_got = copy(PRM_CORE, prm.at[1 - c], prm.at[1 - c], core_dev)

    g_side = copy(G_SIDE, side_out, side_in, side_dev)
    g_hop = [copy(G_HOP + i, hop_out.at[0, part(i)], hop_in.at[0, part(i)], side_dev) for i in two]
    g_far_hop = [copy(G_FAR_HOP + i, hop_out.at[1, part(i)], hop_in.at[1, part(i)], side_dev) for i in two]
    g_back = [copy(G_BACK + i, back_out.at[0, part(i)], back_in.at[0, part(i)], back_dev) for i in two]
    g_relay = {i: copy(G_RELAY + i - back_later[0], back_out.at[0, part(i)], relay.at[1, part(i)], z_back) for i in back_later}
    g_passed = {i: copy(G_BACK + i, relay.at[1, part(i)], back_in.at[0, part(i)], y_back) for i in back_later}
    g_far_z = [copy(G_FAR_Z + i, back_out.at[1, part(i)], relay.at[1, part(i)], z_back) for i in two]
    g_far_passed = [copy(G_FAR + i, relay.at[1, part(i)], back_in.at[1, part(i)], y_back2) for i in two]
    g_far = [copy(G_FAR + i, back_out.at[1, part(i)], back_in.at[1, part(i)], back2_dev) for i in two]
    ig_core = [copy(IG_CORE + i, core_out.at[slot(i)], core_in.at[slot(i)], core_dev) for i in range(4)]
    ig_a = [copy(IG_A + i, img_out.at[0, part(i)], img_in.at[0, part(i)], a_dev) for i in two]
    ig_z = [copy(IG_Z + i, img_out.at[1, part(i)], img_in.at[1, part(i)], z_dev) for i in two]
    ig_az = [
        copy(IG_AZ + i, img_out.at[2, part(i)], img_in.at[2, part(i)], a_dev) for i in two
    ]
    ig_za = [copy(IG_AZ + i, img_out.at[2, part(i)], img_in.at[2, part(i)], z_dev) for i in two]
    free = jnp.logical_not(crowded)
    crowded_back = first | last

    for i in later:
        pl.when(by_z[i])(t_relay[i].start)
    for i in two:
        if i in later:
            pl.when(jnp.logical_not(by_z[i]))(t_next[i].start)
        else:
            t_next[i].start()
    for i in two:
        pl.when(before & (c == 1))(t_far_z[i].start)
        pl.when(last & (c == 1))(t_direct[i].start)
    early, late = two[:HALF], two[HALF:]
    for i, k in zip(early, late):
        img_z[i].start()
        img_a[k].start()
    for i, k in zip(early, late):
        img_z[k].start()
        img_a[i].start()
    for i in range(3):
        params[i].start()
    t_side.start()
    img_core[0].start()
    tg[...] = jnp.zeros_like(tg)
    ig[...] = jnp.zeros_like(ig)

    def pass_relayed():
        for i in later:

            @pl.when(by_z[i])
            def _():
                t_relay[i].wait_recv()
                t_passed[i].start()


    def pass_far_relayed():
        for i in two:
            t_far_z[i].wait_recv()
            t_far_passed[i].start()

    def pass_next():
        for i in two:
            if i == later[0]:
                pl.when(last & jnp.logical_not(lowest))(pass_relayed)
            t_next[i].wait_recv()
            pl.when((c == 1) & jnp.logical_not(last | first))(t_far[i].start)
            t_hop[i].start()
        pl.when(before & jnp.logical_not(lowest) & (c == 1))(pass_far_relayed)

    def pass_far():
        for i in two:
            pl.when(first)(t_far_passed[i].wait_recv)
            pl.when(second)(t_direct[i].wait_recv)
            pl.when(jnp.logical_not(first | second))(t_far[i].wait_recv)
            t_far_hop[i].start()

    for i, k in zip(early, late):
        img_z[i].wait_recv()
        img_az[i].start()
        @pl.when(free)
        def _():
            img_a[k].wait_recv()
            img_za[k].start()

        @pl.when(crowded)
        def _():
            img_z[k].wait_recv()
            img_az[k].start()

    pl.when(jnp.logical_not(first))(pass_next)
    for i in early:
        img_a[i].wait_recv()
    pl.when(free)(img_core[1].start)
    for i in late:
        pl.when(crowded)(img_a[i].wait_recv)
    pl.when(crowded)(img_core[1].start)
    for i in late:
        pl.when(free)(img_z[i].wait_recv)
    img_core[2].start()
    for i in two:
        img_az[i].wait_recv()
    img_core[3].start()
    for i in range(3):
        params[i].wait_recv()
    prm_core.start()
    pl.when(first)(pass_next)
    pl.when(last & lowest)(pass_relayed)
    pl.when(before & lowest & (c == 1))(pass_far_relayed)
    t_side.wait_recv()

    wait = jnp.where(first & (c == 0), 1, 0)

    def tile(s, _):
        j = wait * (s // 2) + (1 - wait) * ((s + 1) // 2 - (s // 3) * (2 - 2 * c))
        other = wait * (s % 2) + (1 - wait) * (s // 2)
        i = c + other * (1 - 2 * c)

        @pl.when(s == 1 + wait)
        def _():
            pl.when((c == 1) & jnp.logical_not(first | (second & lowest)))(pass_far)
            for q in two:
                t_hop[q].wait_recv()

        @pl.when(s == 2 - wait)
        def _():
            for q in range(4):
                img_got[q].wait_recv()
            prm_got.wait_recv()

        @pl.when((s == 2) & (c == 1) & first)
        def _():
            pass_far()

        @pl.when((s == 3) & (c == 1))
        def _():
            pl.when(second & lowest)(pass_far)
            for q in two:
                t_far_hop[q].wait_recv()

        scores = lax.dot_general(tx[j], img[i], (((1,), (1,)), ((), ())), preferred_element_type=F32)
        prob = jnp.exp(scale * scores - prm[i, 0:1, :])
        row = lax.broadcasted_iota(jnp.int32, scores.shape, 0)
        place = jnp.where(row < rows, row.astype(F32) + base_own, (row - rows).astype(F32) + base_side)
        place = place + (s * 65536).astype(F32)
        prob = prob - jnp.where(place == prm[i, 2:3, :], 1.0, 0.0)
        weight = (prob * (scale * prm[i, 1:2, :])).astype(BF16)
        tg[j] += jnp.dot(weight, img[i], preferred_element_type=F32)
        ig[i] += lax.dot_general(weight, tx[j], (((0,), (0,)), ((), ())), preferred_element_type=F32)

        @pl.when((s == 0) & (c == 1))
        def _():
            side_out[...] = tg[0, side].astype(BF16)
            g_side.start()

        @pl.when(s == 2 + wait)
        def _():
            for q in two:
                hop_out[0, part(q)] = tg[1, side_part(q)].astype(BF16)
                g_hop[q].start()

        @pl.when((s == 3) & (c == 1))
        def _():
            for q in two:
                hop_out[1, part(q)] = tg[2, side_part(q)].astype(BF16)
                g_far_hop[q].start()

        return 0

    lax.fori_loop(0, 4, tile, 0)

    for i in (3, 1, 2, 0):
        core_out[slot(i)] = ig[1 - c, slot(i)].astype(BF16)
        ig_core[i].start()

    def ready_part(n, i):
        return ig[c, slot_part(n, i)] + core_in[slot_part(n, i)].astype(F32)

    ig_core[3].wait_recv()
    for i, k in zip(early, late):
        for q in (i, k):
            img_out[2, part(q)] = ready_part(3, q).astype(BF16)
        ig_az[i].start()
        pl.when(crowded_back)(ig_az[k].start)
        pl.when(jnp.logical_not(crowded_back))(ig_za[k].start)
    ig_core[1].wait_recv()
    ig_core[2].wait_recv()
    for i, k in zip(early, late):
        img_out[0, part(i)] = ready_part(1, i).astype(BF16)
        ig_a[i].start()

        @pl.when(jnp.logical_not(crowded_back))
        def _():
            img_out[1, part(k)] = ready_part(2, k).astype(BF16)
            ig_z[k].start()

        @pl.when(crowded_back)
        def _():
            img_out[0, part(k)] = ready_part(1, k).astype(BF16)
            ig_a[k].start()

    for i in two:
        g_hop[i].wait_recv()
        back_out[0, part(i)] = (tg[1, part(i)] + hop_in[0, part(i)].astype(F32)).astype(BF16)
        if i in back_later:
            pl.when(jnp.logical_not(first))(g_back[i].start)

            @pl.when(first)
            def _():
                if i == back_later[0]:
                    pl.semaphore_wait(ready, 1)
                g_relay[i].start()
        else:
            g_back[i].start()

    @pl.when(c == 0)
    def _():
        side_out[...] = tg[0, side].astype(BF16)
        g_side.start()

    def far_back(i):
        @pl.when(c == 1)
        def _():
            g_far_hop[i].wait_recv()
            back_out[1, part(i)] = (tg[2, part(i)] + hop_in[1, part(i)].astype(F32)).astype(BF16)
            pl.when(jnp.logical_not(second))(g_far[i].start)

            @pl.when(second)
            def _():
                if i == 0:
                    pl.semaphore_wait(ready, 1)
                g_far_z[i].start()

    for i, k in zip(early, late):
        far_back(2 * i)
        ig_az[i].wait_recv()
        img_out[1, part(i)] = (ready_part(2, i) + img_in[2, part(i)].astype(F32)).astype(BF16)
        ig_z[i].start()
        far_back(2 * i + 1)
        ig_az[k].wait_recv()

        @pl.when(jnp.logical_not(crowded_back))
        def _():
            img_out[0, part(k)] = (ready_part(1, k) + img_in[2, part(k)].astype(F32)).astype(BF16)
            ig_a[k].start()

        @pl.when(crowded_back)
        def _():
            img_out[1, part(k)] = (ready_part(2, k) + img_in[2, part(k)].astype(F32)).astype(BF16)
            ig_z[k].start()

    for sent in (t_side, *t_next, *t_hop, *img_a, *img_z, *img_az, *params, *img_core, prm_core, g_side, *g_hop, *ig_core):
        sent.wait_send()
    for i in later:
        pl.when(by_z[i])(t_relay[i].wait_send)

    @pl.when(c == 1)
    def _():
        for sent in (*t_far_hop, *g_far_hop):
            sent.wait_send()
        for i in two:
            pl.when(jnp.logical_not(last | first))(t_far[i].wait_send)
            pl.when(last)(t_direct[i].wait_send)
            pl.when(before)(t_far_z[i].wait_send)
            pl.when(before)(t_far_passed[i].wait_send)

    @pl.when(first)
    def _():
        for i in back_later:
            g_relay[i].wait_recv()
            g_passed[i].start()

    @pl.when(second & (c == 1))
    def _():
        for i in two:
            g_far_z[i].wait_recv()
            g_far_passed[i].start()

    ig_core[0].wait_recv()
    ig[c, own] += core_in[own].astype(F32)
    g_side.wait_recv()
    tg[0, own] += side_in[...].astype(F32)

    for i in two:
        ig_a[i].wait_recv()
        ig_z[i].wait_recv()
    image_vm[...] = ((ig[c, own] + img_in[0].astype(F32)) + img_in[1].astype(F32)).astype(BF16)

    image_store = pltpu.make_async_copy(image_vm, image_out, load_sem.at[0])
    image_store.start()
    for sent in (*g_back, *ig_a, *ig_z, *ig_az):
        sent.wait_send()
    for i in back_later:
        pl.when(first)(g_relay[i].wait_send)

    @pl.when(c == 1)
    def _():
        for sent in g_far:
            sent.wait_send()
        for sent in g_far_z:
            pl.when(second)(sent.wait_send)

    for i in two:
        g_back[i].wait_recv()

    @pl.when(c == 0)
    def _():
        text_vm[...] = (tg[0, own] + back_in[0].astype(F32)).astype(BF16)

    @pl.when(c == 1)
    def _():
        for i in two:
            g_far[i].wait_recv()
        text_vm[...] = ((tg[0, own] + back_in[0].astype(F32)) + back_in[1].astype(F32)).astype(BF16)

    text_store = pltpu.make_async_copy(text_vm, text_out, load_sem.at[1])
    text_store.start()

    image_store.wait()
    text_store.wait()


def hand_over(image_ref, text_ref, image_out, text_out, held, load_sem, store_sem):
    half = image_ref.shape[0] // 4
    pieces = [(n, i) for n in range(2) for i in range(4)]
    loads, stores = [], []
    for n, i in pieces:
        rows = pl.ds(i * half, half)
        source, target = (image_ref, image_out) if n == 0 else (text_ref, text_out)
        k = 4 * n + i
        loads.append(pltpu.make_async_copy(source.at[rows], held.at[k], load_sem.at[k]))
        stores.append(pltpu.make_async_copy(held.at[k], target.at[rows], store_sem.at[k]))
    for load in loads:
        load.start()
    for load, store in zip(loads, stores):
        load.wait()
        store.start()
    for store in stores:
        store.wait()


def solution(mesh):
    n_blk = mesh.shape["blk"]

    def per_device(image_rows, text_rows, log_norm, row_grad, pos_index, logit_scale):
        rows, width = image_rows.shape
        anywhere = pl.BlockSpec(memory_space=pltpu.HBM)
        grads = pl.pallas_call(
            functools.partial(kernel, n_blk),
            out_shape=(jax.ShapeDtypeStruct((rows, width), BF16),) * 2,
            in_specs=[pl.BlockSpec(memory_space=pltpu.SMEM)] + [anywhere] * 5,
            out_specs=(anywhere,) * 2,
            scratch_shapes=[
                pltpu.VMEM((2, 4 * rows, width), BF16),
                pltpu.VMEM((2, 8, 4 * rows), F32),
                pltpu.VMEM((3, 2 * rows, width), BF16),
                pltpu.VMEM((2, 1, rows), F32),
                pltpu.VMEM((1, rows), jnp.int32),
                pltpu.VMEM((3, 2 * rows, width), F32),
                pltpu.VMEM((2, 4 * rows, width), F32),
                pltpu.VMEM((4 * rows, width), BF16),
                pltpu.VMEM((4 * rows, width), BF16),
                pltpu.VMEM((rows, width), BF16),
                pltpu.VMEM((rows, width), BF16),
                pltpu.VMEM((2, rows, width), BF16),
                pltpu.VMEM((2, rows, width), BF16),
                pltpu.VMEM((2, rows, width), BF16),
                pltpu.VMEM((2, rows, width), BF16),
                pltpu.VMEM((3, rows, width), BF16),
                pltpu.VMEM((3, rows, width), BF16),
                pltpu.VMEM((2, rows, width), BF16),
                pltpu.VMEM((rows, width), BF16),
                pltpu.VMEM((rows, width), BF16),
                pltpu.SemaphoreType.DMA((5,)),
                pltpu.SemaphoreType.DMA((N_COPIES,)),
                pltpu.SemaphoreType.DMA((N_COPIES,)),
                pltpu.SemaphoreType.REGULAR,
            ],
            compiler_params=pltpu.CompilerParams(
                collective_id=0, has_side_effects=True, vmem_limit_bytes=60 * 2**20
            ),
            name="window_loss_grad",
        )(
            logit_scale.reshape(1, 1), image_rows, text_rows, log_norm.reshape(1, rows),
            row_grad.reshape(1, rows), pos_index.reshape(1, rows),
        )
        return pl.pallas_call(
            hand_over,
            out_shape=(jax.ShapeDtypeStruct((rows, width), BF16),) * 2,
            in_specs=[anywhere] * 2,
            out_specs=(anywhere,) * 2,
            scratch_shapes=[
                pltpu.VMEM((8, rows // 4, width), BF16),
                pltpu.SemaphoreType.DMA((8,)),
                pltpu.SemaphoreType.DMA((8,)),
            ],
            compiler_params=pltpu.CompilerParams(vmem_limit_bytes=60 * 2**20),
            name="hand_over",
        )(*grads)

    return jax.shard_map(
        per_device,
        mesh=mesh,
        in_specs=(
            P(("blk", "group"), None),
            P(("blk", "group"), None),
            P(("blk", "group")),
            P(("blk", "group")),
            P(("blk", "group")),
            P(),
        ),
        out_specs=(P(("blk", "group"), None), P(("blk", "group"), None)),
        check_vma=False,
    )
```

```python
import functools

import jax
import jax.numpy as jnp
from jax import lax
from jax.experimental import pallas as pl
from jax.experimental.pallas import tpu as pltpu
from jax.sharding import PartitionSpec as P

MESH = pl.DeviceIdType.MESH
F32 = jnp.float32
BF16 = jnp.bfloat16
PIECES = 4
LATER = 2
BACK_LATER = 1
Y = 8

HALF = PIECES // 2

T_SIDE = 0
T_NEXT = 1
T_HOP = T_NEXT + PIECES
T_FAR = T_HOP + PIECES
T_FAR_HOP = T_FAR + PIECES
IMG = T_FAR_HOP + PIECES
IMG_Z = IMG + PIECES
IMG_AZ = IMG_Z + PIECES
PRM = IMG_AZ + PIECES
IMG_CORE = PRM + 3
PRM_CORE = IMG_CORE + 4
G_SIDE = PRM_CORE + 1
G_HOP = G_SIDE + 1
G_BACK = G_HOP + PIECES
G_FAR_HOP = G_BACK + PIECES
G_FAR = G_FAR_HOP + PIECES
IG_CORE = G_FAR + PIECES
IG_A = IG_CORE + 4
IG_Z = IG_A + PIECES
IG_AZ = IG_Z + PIECES
T_RELAY = IG_AZ + PIECES
G_RELAY = T_RELAY + LATER
T_FAR_Z = G_RELAY + BACK_LATER
T_FAR_PASSED = T_FAR_Z + PIECES
G_FAR_Z = T_FAR_PASSED + PIECES
T_DIRECT = G_FAR_Z + PIECES
T_PASSED = T_DIRECT + PIECES
N_COPIES = T_PASSED


def kernel(n_blk, scale_ref, image_ref, text_ref, log_ref, grad_ref, pos_ref, image_out, text_out,
           img, prm, tx, rowv, posv, tg, ig, core_out, core_in, side_out, side_in, hop_out, hop_in,
           back_out, back_in, img_out, img_in, relay, image_vm, text_vm, load_sem, send_sem, recv_sem, ready):
    rows = image_ref.shape[0]
    piece = rows // PIECES
    blk, grp = lax.axis_index("blk"), lax.axis_index("group")
    c = blk % 2
    pair = blk // 2
    n_pair = n_blk // 2
    z, x = grp // 4, grp % 4
    x_a = x + 1 - 2 * (x % 2)
    x_b = 3 - x

    def at_pair(step):
        return (((pair + step + n_pair) % n_pair) * 2 + c, grp)

    core_dev = (pair * 2 + 1 - c, grp)
    side_dev = (blk, z * 4 + x_b)
    a_dev, z_dev = (blk, z * 4 + x_a), (blk, (1 - z) * 4 + x)
    img_devs = (a_dev, z_dev, (blk, (1 - z) * 4 + x_a))
    next_dev, back_dev = at_pair(1), at_pair(-1)
    next2_dev, back2_dev = at_pair(2), at_pair(-2)
    y = pair % Y
    last, first, before, second = y == Y - 1, y == 0, y == Y - 2, y == 1
    crowded = first
    lowest = pair < Y
    z_next, z_back = at_pair(Y), at_pair(-Y)
    y_next, y_back = at_pair((y + 1) % Y - y), at_pair((y + Y - 1) % Y - y)
    y_next2, y_back2 = at_pair((y + 2) % Y - y), at_pair((y + Y - 2) % Y - y)

    own, side = pl.ds(0, rows), pl.ds(rows, rows)

    def slot(i):
        return pl.ds(i * rows, rows)

    def part(i):
        return pl.ds(i * piece, piece)

    def slot_part(s, i):
        return pl.ds(s * rows + i * piece, piece)

    def side_part(i):
        return slot_part(1, i)

    def copy(index, src, dst, device):
        return pltpu.make_async_remote_copy(
            src_ref=src, dst_ref=dst, send_sem=send_sem.at[index], recv_sem=recv_sem.at[index],
            device_id=device, device_id_type=MESH,
        )

    loads = [
        pltpu.make_async_copy(text_ref, tx.at[0, own], load_sem.at[0]),
        pltpu.make_async_copy(image_ref, img.at[c, own], load_sem.at[1]),
        pltpu.make_async_copy(log_ref, rowv.at[0], load_sem.at[2]),
        pltpu.make_async_copy(grad_ref, rowv.at[1], load_sem.at[3]),
        pltpu.make_async_copy(pos_ref, posv, load_sem.at[4]),
    ]
    barrier = pltpu.get_barrier_semaphore()
    senders = (core_dev, side_dev, *img_devs, back_dev)
    for device in senders:
        pl.semaphore_signal(barrier, inc=1, device_id=device, device_id_type=MESH)

    @pl.when(last | before | first | second)
    def _():
        pl.semaphore_signal(barrier, inc=1, device_id=z_back, device_id_type=MESH)

    @pl.when(first)
    def _():
        pl.semaphore_signal(barrier, inc=1, device_id=y_back, device_id_type=MESH)
        pl.semaphore_signal(barrier, inc=1, device_id=y_back2, device_id_type=MESH)

    @pl.when(second)
    def _():
        pl.semaphore_signal(barrier, inc=1, device_id=back2_dev, device_id_type=MESH)

    for load in loads:
        load.start()
    for load in loads:
        load.wait()
    prm[c, 0:1, 0:rows] = rowv[0]
    prm[c, 1:2, 0:rows] = rowv[1]
    prm[c, 2:3, 0:rows] = posv[...].astype(F32)
    prm[c, 3:8, 0:rows] = jnp.zeros((5, rows), F32)
    pl.semaphore_wait(barrier, len(senders) + jnp.where(last, 3, jnp.where(before, 2, jnp.where(first | second, 1, 0))))

    @pl.when(first | (second & (c == 1)))
    def _():
        pl.semaphore_signal(ready, inc=1, device_id=z_next, device_id_type=MESH)

    scale = scale_ref[0, 0]
    base_own = (grp * rows).astype(F32)
    base_side = ((z * 4 + x_b) * rows).astype(F32)
    two = range(PIECES)

    t_side = copy(T_SIDE, tx.at[0, own], tx.at[0, side], side_dev)
    t_next = [copy(T_NEXT + i, tx.at[0, part(i)], tx.at[1, part(i)], next_dev) for i in two]
    later = range(PIECES - LATER, PIECES)
    by_z = {i: last & ((z == 1) | (i == later[-1])) for i in later}
    back_later = range(BACK_LATER)
    t_relay = {i: copy(T_RELAY + i - later[0], tx.at[0, part(i)], relay.at[0, part(i)], z_next) for i in later}
    t_passed = {i: copy(T_NEXT + i, relay.at[0, part(i)], tx.at[1, part(i)], y_next) for i in later}
    t_far_z = [copy(T_FAR_Z + i, tx.at[0, part(i)], relay.at[0, part(i)], z_next) for i in two]
    t_far_passed = [copy(T_FAR_PASSED + i, relay.at[0, part(i)], tx.at[2, part(i)], y_next2) for i in two]
    t_direct = [copy(T_DIRECT + i, tx.at[0, part(i)], tx.at[2, part(i)], next2_dev) for i in two]
    t_hop = [copy(T_HOP + i, tx.at[1, part(i)], tx.at[1, side_part(i)], side_dev) for i in two]
    t_far = [copy(T_FAR + i, tx.at[1, part(i)], tx.at[2, part(i)], next_dev) for i in two]
    t_far_hop = [copy(T_FAR_HOP + i, tx.at[2, part(i)], tx.at[2, side_part(i)], side_dev) for i in two]
    img_a = [copy(IMG + i, img.at[c, part(i)], img.at[c, slot_part(1, i)], a_dev) for i in two]
    img_z = [copy(IMG_Z + i, img.at[c, part(i)], img.at[c, slot_part(2, i)], z_dev) for i in two]
    img_az = [
        copy(IMG_AZ + i, img.at[c, slot_part(2, i)], img.at[c, slot_part(3, i)], a_dev) for i in two
    ]
    img_za = [copy(IMG_AZ + i, img.at[c, slot_part(1, i)], img.at[c, slot_part(3, i)], z_dev) for i in two]
    params = [copy(PRM + i, prm.at[c, :, own], prm.at[c, :, slot(i + 1)], img_devs[i]) for i in range(3)]
    img_core = [copy(IMG_CORE + i, img.at[c, slot(i)], img.at[c, slot(i)], core_dev) for i in range(4)]
    prm_core = copy(PRM_CORE, prm.at[c], prm.at[c], core_dev)
    img_got = [copy(IMG_CORE + i, img.at[1 - c, slot(i)], img.at[1 - c, slot(i)], core_dev) for i in range(4)]
    prm_got = copy(PRM_CORE, prm.at[1 - c], prm.at[1 - c], core_dev)

    g_side = copy(G_SIDE, side_out, side_in, side_dev)
    g_hop = [copy(G_HOP + i, hop_out.at[0, part(i)], hop_in.at[0, part(i)], side_dev) for i in two]
    g_far_hop = [copy(G_FAR_HOP + i, hop_out.at[1, part(i)], hop_in.at[1, part(i)], side_dev) for i in two]
    g_back = [copy(G_BACK + i, back_out.at[0, part(i)], back_in.at[0, part(i)], back_dev) for i in two]
    g_relay = {i: copy(G_RELAY + i - back_later[0], back_out.at[0, part(i)], relay.at[1, part(i)], z_back) for i in back_later}
    g_passed = {i: copy(G_BACK + i, relay.at[1, part(i)], back_in.at[0, part(i)], y_back) for i in back_later}
    g_far_z = [copy(G_FAR_Z + i, back_out.at[1, part(i)], relay.at[1, part(i)], z_back) for i in two]
    g_far_passed = [copy(G_FAR + i, relay.at[1, part(i)], back_in.at[1, part(i)], y_back2) for i in two]
    g_far = [copy(G_FAR + i, back_out.at[1, part(i)], back_in.at[1, part(i)], back2_dev) for i in two]
    ig_core = [copy(IG_CORE + i, core_out.at[slot(i)], core_in.at[slot(i)], core_dev) for i in range(4)]
    ig_a = [copy(IG_A + i, img_out.at[0, part(i)], img_in.at[0, part(i)], a_dev) for i in two]
    ig_z = [copy(IG_Z + i, img_out.at[1, part(i)], img_in.at[1, part(i)], z_dev) for i in two]
    ig_az = [
        copy(IG_AZ + i, img_out.at[2, part(i)], img_in.at[2, part(i)], a_dev) for i in two
    ]
    ig_za = [copy(IG_AZ + i, img_out.at[2, part(i)], img_in.at[2, part(i)], z_dev) for i in two]
    free = jnp.logical_not(crowded)
    crowded_back = first | last

    for i in later:
        pl.when(by_z[i])(t_relay[i].start)
    for i in two:
        if i in later:
            pl.when(jnp.logical_not(by_z[i]))(t_next[i].start)
        else:
            t_next[i].start()
    for i in two:
        pl.when(before & (c == 1))(t_far_z[i].start)
        pl.when(last & (c == 1))(t_direct[i].start)
    early, late = two[:HALF], two[HALF:]
    for i, k in zip(early, late):
        img_z[i].start()
        img_a[k].start()
    for i, k in zip(early, late):
        img_z[k].start()
        img_a[i].start()
    for i in range(3):
        params[i].start()
    t_side.start()
    img_core[0].start()
    tg[...] = jnp.zeros_like(tg)
    ig[...] = jnp.zeros_like(ig)

    def pass_relayed():
        for i in later:

            @pl.when(by_z[i])
            def _():
                t_relay[i].wait_recv()
                t_passed[i].start()


    def pass_far_relayed():
        for i in two:
            t_far_z[i].wait_recv()
            t_far_passed[i].start()

    def pass_next():
        for i in two:
            if i == later[0]:
                pl.when(last & jnp.logical_not(lowest))(pass_relayed)
            t_next[i].wait_recv()
            pl.when((c == 1) & jnp.logical_not(last | first))(t_far[i].start)
            t_hop[i].start()
        pl.when(before & jnp.logical_not(lowest) & (c == 1))(pass_far_relayed)

    def pass_far():
        for i in two:
            pl.when(first)(t_far_passed[i].wait_recv)
            pl.when(second)(t_direct[i].wait_recv)
            pl.when(jnp.logical_not(first | second))(t_far[i].wait_recv)
            t_far_hop[i].start()

    for i, k in zip(early, late):
        img_z[i].wait_recv()
        img_az[i].start()
        @pl.when(free)
        def _():
            img_a[k].wait_recv()
            img_za[k].start()

        @pl.when(crowded)
        def _():
            img_z[k].wait_recv()
            img_az[k].start()

    pl.when(jnp.logical_not(first))(pass_next)
    for i in early:
        img_a[i].wait_recv()
    pl.when(free)(img_core[1].start)
    for i in late:
        pl.when(crowded)(img_a[i].wait_recv)
    pl.when(crowded)(img_core[1].start)
    for i in late:
        pl.when(free)(img_z[i].wait_recv)
    img_core[2].start()
    for i in two:
        img_az[i].wait_recv()
    img_core[3].start()
    for i in range(3):
        params[i].wait_recv()
    prm_core.start()
    pl.when(first)(pass_next)
    pl.when(last & lowest)(pass_relayed)
    pl.when(before & lowest & (c == 1))(pass_far_relayed)
    t_side.wait_recv()

    wait = jnp.where(first & (c == 0), 1, 0)

    def tile(s, _):
        j = wait * (s // 2) + (1 - wait) * ((s + 1) // 2 - (s // 3) * (2 - 2 * c))
        other = wait * (s % 2) + (1 - wait) * (s // 2)
        i = c + other * (1 - 2 * c)

        @pl.when(s == 1 + wait)
        def _():
            pl.when((c == 1) & jnp.logical_not(first | (second & lowest)))(pass_far)
            for q in two:
                t_hop[q].wait_recv()

        @pl.when(s == 2 - wait)
        def _():
            for q in range(4):
                img_got[q].wait_recv()
            prm_got.wait_recv()

        @pl.when((s == 2) & (c == 1) & first)
        def _():
            pass_far()

        @pl.when((s == 3) & (c == 1))
        def _():
            pl.when(second & lowest)(pass_far)
            for q in two:
                t_far_hop[q].wait_recv()

        scores = lax.dot_general(tx[j], img[i], (((1,), (1,)), ((), ())), preferred_element_type=F32)
        prob = jnp.exp(scale * scores - prm[i, 0:1, :])
        row = lax.broadcasted_iota(jnp.int32, scores.shape, 0)
        place = jnp.where(row < rows, row.astype(F32) + base_own, (row - rows).astype(F32) + base_side)
        place = place + (s * 65536).astype(F32)
        prob = prob - jnp.where(place == prm[i, 2:3, :], 1.0, 0.0)
        weight = (prob * (scale * prm[i, 1:2, :])).astype(BF16)
        tg[j] += jnp.dot(weight, img[i], preferred_element_type=F32)
        ig[i] += lax.dot_general(weight, tx[j], (((0,), (0,)), ((), ())), preferred_element_type=F32)

        @pl.when((s == 0) & (c == 1))
        def _():
            side_out[...] = tg[0, side].astype(BF16)
            g_side.start()

        @pl.when(s == 2 + wait)
        def _():
            for q in two:
                hop_out[0, part(q)] = tg[1, side_part(q)].astype(BF16)
                g_hop[q].start()

        @pl.when((s == 3) & (c == 1))
        def _():
            for q in two:
                hop_out[1, part(q)] = tg[2, side_part(q)].astype(BF16)
                g_far_hop[q].start()

        return 0

    lax.fori_loop(0, 4, tile, 0)

    for i in (3, 1, 2, 0):
        core_out[slot(i)] = ig[1 - c, slot(i)].astype(BF16)
        ig_core[i].start()

    def ready_part(n, i):
        return ig[c, slot_part(n, i)] + core_in[slot_part(n, i)].astype(F32)

    ig_core[3].wait_recv()
    for i, k in zip(early, late):
        for q in (i, k):
            img_out[2, part(q)] = ready_part(3, q).astype(BF16)
        ig_az[i].start()
        pl.when(crowded_back)(ig_az[k].start)
        pl.when(jnp.logical_not(crowded_back))(ig_za[k].start)
    ig_core[1].wait_recv()
    ig_core[2].wait_recv()
    for i, k in zip(early, late):
        img_out[0, part(i)] = ready_part(1, i).astype(BF16)
        ig_a[i].start()

        @pl.when(jnp.logical_not(crowded_back))
        def _():
            img_out[1, part(k)] = ready_part(2, k).astype(BF16)
            ig_z[k].start()

        @pl.when(crowded_back)
        def _():
            img_out[0, part(k)] = ready_part(1, k).astype(BF16)
            ig_a[k].start()

    for i in two:
        g_hop[i].wait_recv()
        back_out[0, part(i)] = (tg[1, part(i)] + hop_in[0, part(i)].astype(F32)).astype(BF16)
        if i in back_later:
            pl.when(jnp.logical_not(first))(g_back[i].start)

            @pl.when(first)
            def _():
                if i == back_later[0]:
                    pl.semaphore_wait(ready, 1)
                g_relay[i].start()
        else:
            g_back[i].start()

    @pl.when(c == 0)
    def _():
        side_out[...] = tg[0, side].astype(BF16)
        g_side.start()

    def far_back(i):
        @pl.when(c == 1)
        def _():
            g_far_hop[i].wait_recv()
            back_out[1, part(i)] = (tg[2, part(i)] + hop_in[1, part(i)].astype(F32)).astype(BF16)
            pl.when(jnp.logical_not(second))(g_far[i].start)

            @pl.when(second)
            def _():
                if i == 0:
                    pl.semaphore_wait(ready, 1)
                g_far_z[i].start()

    for i, k in zip(early, late):
        far_back(2 * i)
        ig_az[i].wait_recv()
        img_out[1, part(i)] = (ready_part(2, i) + img_in[2, part(i)].astype(F32)).astype(BF16)
        ig_z[i].start()
        far_back(2 * i + 1)
        ig_az[k].wait_recv()

        @pl.when(jnp.logical_not(crowded_back))
        def _():
            img_out[0, part(k)] = (ready_part(1, k) + img_in[2, part(k)].astype(F32)).astype(BF16)
            ig_a[k].start()

        @pl.when(crowded_back)
        def _():
            img_out[1, part(k)] = (ready_part(2, k) + img_in[2, part(k)].astype(F32)).astype(BF16)
            ig_z[k].start()

    @pl.when(first)
    def _():
        for i in back_later:
            g_relay[i].wait_recv()
            g_passed[i].start()

    @pl.when(second & (c == 1))
    def _():
        for i in two:
            g_far_z[i].wait_recv()
            g_far_passed[i].start()

    for sent in (t_side, *t_next, *t_hop, *img_a, *img_z, *img_az, *params, *img_core, prm_core, g_side, *g_hop, *ig_core):
        sent.wait_send()
    for i in later:
        pl.when(by_z[i])(t_relay[i].wait_send)

    @pl.when(c == 1)
    def _():
        for sent in (*t_far_hop, *g_far_hop):
            sent.wait_send()
        for i in two:
            pl.when(jnp.logical_not(last | first))(t_far[i].wait_send)
            pl.when(last)(t_direct[i].wait_send)
            pl.when(before)(t_far_z[i].wait_send)
            pl.when(before)(t_far_passed[i].wait_send)

    ig_core[0].wait_recv()
    ig[c, own] += core_in[own].astype(F32)
    g_side.wait_recv()
    tg[0, own] += side_in[...].astype(F32)

    for i in two:
        ig_a[i].wait_recv()
        ig_z[i].wait_recv()
    image_vm[...] = ((ig[c, own] + img_in[0].astype(F32)) + img_in[1].astype(F32)).astype(BF16)

    image_store = pltpu.make_async_copy(image_vm, image_out, load_sem.at[0])
    image_store.start()
    for sent in (*g_back, *ig_a, *ig_z, *ig_az):
        sent.wait_send()
    for i in back_later:
        pl.when(first)(g_relay[i].wait_send)

    @pl.when(c == 1)
    def _():
        for sent in g_far:
            sent.wait_send()
        for sent in g_far_z:
            pl.when(second)(sent.wait_send)

    for i in two:
        g_back[i].wait_recv()

    @pl.when(c == 0)
    def _():
        text_vm[...] = (tg[0, own] + back_in[0].astype(F32)).astype(BF16)

    @pl.when(c == 1)
    def _():
        for i in two:
            g_far[i].wait_recv()
        text_vm[...] = ((tg[0, own] + back_in[0].astype(F32)) + back_in[1].astype(F32)).astype(BF16)

    text_store = pltpu.make_async_copy(text_vm, text_out, load_sem.at[1])
    text_store.start()

    image_store.wait()
    text_store.wait()


def hand_over(image_ref, text_ref, image_out, text_out, held, load_sem, store_sem):
    half = image_ref.shape[0] // 4
    pieces = [(n, i) for n in range(2) for i in range(4)]
    loads, stores = [], []
    for n, i in pieces:
        rows = pl.ds(i * half, half)
        source, target = (image_ref, image_out) if n == 0 else (text_ref, text_out)
        k = 4 * n + i
        loads.append(pltpu.make_async_copy(source.at[rows], held.at[k], load_sem.at[k]))
        stores.append(pltpu.make_async_copy(held.at[k], target.at[rows], store_sem.at[k]))
    for load in loads:
        load.start()
    for load, store in zip(loads, stores):
        load.wait()
        store.start()
    for store in stores:
        store.wait()


def solution(mesh):
    n_blk = mesh.shape["blk"]

    def per_device(image_rows, text_rows, log_norm, row_grad, pos_index, logit_scale):
        rows, width = image_rows.shape
        anywhere = pl.BlockSpec(memory_space=pltpu.HBM)
        grads = pl.pallas_call(
            functools.partial(kernel, n_blk),
            out_shape=(jax.ShapeDtypeStruct((rows, width), BF16),) * 2,
            in_specs=[pl.BlockSpec(memory_space=pltpu.SMEM)] + [anywhere] * 5,
            out_specs=(anywhere,) * 2,
            scratch_shapes=[
                pltpu.VMEM((2, 4 * rows, width), BF16),
                pltpu.VMEM((2, 8, 4 * rows), F32),
                pltpu.VMEM((3, 2 * rows, width), BF16),
                pltpu.VMEM((2, 1, rows), F32),
                pltpu.VMEM((1, rows), jnp.int32),
                pltpu.VMEM((3, 2 * rows, width), F32),
                pltpu.VMEM((2, 4 * rows, width), F32),
                pltpu.VMEM((4 * rows, width), BF16),
                pltpu.VMEM((4 * rows, width), BF16),
                pltpu.VMEM((rows, width), BF16),
                pltpu.VMEM((rows, width), BF16),
                pltpu.VMEM((2, rows, width), BF16),
                pltpu.VMEM((2, rows, width), BF16),
                pltpu.VMEM((2, rows, width), BF16),
                pltpu.VMEM((2, rows, width), BF16),
                pltpu.VMEM((3, rows, width), BF16),
                pltpu.VMEM((3, rows, width), BF16),
                pltpu.VMEM((2, rows, width), BF16),
                pltpu.VMEM((rows, width), BF16),
                pltpu.VMEM((rows, width), BF16),
                pltpu.SemaphoreType.DMA((5,)),
                pltpu.SemaphoreType.DMA((N_COPIES,)),
                pltpu.SemaphoreType.DMA((N_COPIES,)),
                pltpu.SemaphoreType.REGULAR,
            ],
            compiler_params=pltpu.CompilerParams(
                collective_id=0, has_side_effects=True, vmem_limit_bytes=60 * 2**20
            ),
            name="window_loss_grad",
        )(
            logit_scale.reshape(1, 1), image_rows, text_rows, log_norm.reshape(1, rows),
            row_grad.reshape(1, rows), pos_index.reshape(1, rows),
        )
        return pl.pallas_call(
            hand_over,
            out_shape=(jax.ShapeDtypeStruct((rows, width), BF16),) * 2,
            in_specs=[anywhere] * 2,
            out_specs=(anywhere,) * 2,
            scratch_shapes=[
                pltpu.VMEM((8, rows // 4, width), BF16),
                pltpu.SemaphoreType.DMA((8,)),
                pltpu.SemaphoreType.DMA((8,)),
            ],
            compiler_params=pltpu.CompilerParams(vmem_limit_bytes=60 * 2**20),
            name="hand_over",
        )(*grads)

    return jax.shard_map(
        per_device,
        mesh=mesh,
        in_specs=(
            P(("blk", "group"), None),
            P(("blk", "group"), None),
            P(("blk", "group")),
            P(("blk", "group")),
            P(("blk", "group")),
            P(),
        ),
        out_specs=(P(("blk", "group"), None), P(("blk", "group"), None)),
        check_vma=False,
    )
```
